512 devices in a mesh: gx: 32 (over z, y_hi, core), gy: 16 (over y_lo, x).
Axes of the slice: x: 4, y: 8 (y_hi: 2, y_lo: 4; y = y_hi * 4 + y_lo), z: 8, core: 2. Of those that a mesh axis runs over, the one named last changes fastest.
Arguments:
- forward_state: float32 [9, 256, 256, 128], P(None, 'gx', 'gy'), may hold values from -6 to 6
- adjoint_state: float32 [9, 256, 256, 128], P(None, 'gx', 'gy'), may hold values from -6 to 6
- lame_lambda: float32 [256, 256, 128], P('gx', 'gy'), may hold values from 0.5 to 1.5
- lame_mu: float32 [256, 256, 128], P('gx', 'gy'), may hold values from 0.3 to 1
- buoyancy: float32 [256, 256, 128], P('gx', 'gy'), may hold values from 0.5 to 1
- source_x: int32 [8], replicated, may hold values from 0 to 255
- source_y: int32 [8], replicated, may hold values from 0 to 255
- source_z: int32 [8], replicated, may hold values from 0 to 127
- source_wavelet: float32 [8], replicated, may hold values from -16 to 16
- receiver_x: int32 [256], replicated, may hold values from 0 to 255
- receiver_y: int32 [256], replicated, may hold values from 0 to 255
- receiver_residual: float32 [2, 256], replicated, may hold values from -16 to 16
- absorb_width: int32 [1], replicated, may hold values from 8 to 16
Outputs:
- grad_lambda: float32 [256, 256, 128], P('gx', 'gy')
- grad_mu: float32 [256, 256, 128], P('gx', 'gy')
- grad_density: float32 [256, 256, 128], P('gx', 'gy')
The draws below stay inside these ranges and needn't reach their ends.
All inputs are finite; a program needn't handle non-finite values.
Results may differ from the reference program's by a relative error of at most 0.00002.
Values sent between devices are 32-bit elements; how exact they have to be, the bound alone decides.
A program may use at most 64 MiB of HBM per device.

```python
import math
import jax
import jax.numpy as jnp
from jax import lax

NSRC = 8
NREC = 256
REC_DEPTH = 6
NX = 256
NY = 256
NZ = 128


def with_ends(entries, key, least, high):
    index_at = [jax.random.randint(jax.random.fold_in(key, axis), (), 0, length) for axis, length in enumerate(entries.shape)]
    widest = entries.shape.index(max(entries.shape))
    beside = index_at[:widest] + [(index_at[widest] + 1) % entries.shape[widest]] + index_at[widest + 1:]
    return entries.at[tuple(index_at)].set(least).at[tuple(beside)].set(high)


def steps_of(key, dims, pieces, smallest, high):
    level = 1.0
    for dim, blocks in pieces:
        steps = jax.random.uniform(jax.random.fold_in(jax.random.fold_in(key, 6), dim), (blocks,), jnp.float32, smallest / len(pieces), high / len(pieces))
        level = level * jnp.repeat(jnp.exp(steps), dims[dim] // blocks).reshape((-1,) + (1,) * (len(dims) - 1 - dim))
    return level


def noise(key, shape, deviation, limit, pieces=(), kind=jnp.bfloat16):
    level = steps_of(key, shape, pieces, -0.22, 0.18) if pieces else 1.0
    values = jax.random.normal(key, shape, jnp.float32) * deviation * level
    return jnp.minimum(jnp.maximum(values, -limit), limit).astype(kind)


def setup_inputs(seed: int = 0) -> dict:
    arg_keys = jax.random.split(jax.random.key(seed), 14)
    forward_state = noise(arg_keys[0], (9, NX, NY, NZ), 1.0, 6.0, ((1, 32), (2, 16)), jnp.float32)
    adjoint_state = noise(arg_keys[1], (9, NX, NY, NZ), 1.0, 6.0, ((1, 32), (2, 16)), jnp.float32)
    lame_lambda = jnp.clip(0.5 + 1.0 * jax.random.uniform(arg_keys[2], (NX, NY, NZ), jnp.float32) ** steps_of(arg_keys[2], (NX, NY, NZ), ((0, 32), (1, 16)), -0.2, 0.2), 0.5, 1.5)
    lame_mu = jnp.clip(jnp.exp(math.log(1.0) - 1.2039728 * jax.random.uniform(arg_keys[3], (NX, NY, NZ), jnp.float32) ** steps_of(arg_keys[3], (NX, NY, NZ), ((0, 32), (1, 16)), -0.2, 0.2)), 0.3, 1.0)
    buoyancy = jnp.clip(0.5 + 0.5 * jax.random.uniform(arg_keys[4], (NX, NY, NZ), jnp.float32) ** steps_of(arg_keys[4], (NX, NY, NZ), ((0, 32), (1, 16)), -0.2, 0.2), 0.5, 1.0)
    source_x = with_ends(jax.random.randint(arg_keys[5], (NSRC,), 0, NX), jax.random.fold_in(arg_keys[5], 1), 0, NX - 1).astype(jnp.int32)
    source_y = with_ends(jax.random.randint(arg_keys[6], (NSRC,), 0, NY), jax.random.fold_in(arg_keys[6], 1), 0, NY - 1).astype(jnp.int32)
    source_z = with_ends(jax.random.randint(arg_keys[7], (NSRC,), 0, NZ), jax.random.fold_in(arg_keys[7], 1), 0, NZ - 1).astype(jnp.int32)
    source_wavelet = noise(arg_keys[8], (NSRC,), 4.0, 16.0, (), jnp.float32)
    receiver_x = with_ends(jax.random.randint(arg_keys[9], (NREC,), 0, NX), jax.random.fold_in(arg_keys[9], 1), 0, NX - 1).astype(jnp.int32)
    receiver_y = with_ends(jax.random.randint(arg_keys[10], (NREC,), 0, NY), jax.random.fold_in(arg_keys[10], 1), 0, NY - 1).astype(jnp.int32)
    receiver_residual = noise(arg_keys[11], (2, NREC), 4.0, 16.0, (), jnp.float32)
    absorb_width = jax.random.randint(arg_keys[12], (1,), 8, 17).astype(jnp.int32)
    return {"forward_state": forward_state, "adjoint_state": adjoint_state, "lame_lambda": lame_lambda, "lame_mu": lame_mu, "buoyancy": buoyancy, "source_x": source_x, "source_y": source_y, "source_z": source_z, "source_wavelet": source_wavelet, "receiver_x": receiver_x, "receiver_y": receiver_y, "receiver_residual": receiver_residual, "absorb_width": absorb_width}


COEFS = (1225.0 / 1024.0, -245.0 / 3072.0, 49.0 / 5120.0, -5.0 / 7168.0)
TIME_STEP = 0.2
DAMPING = 0.3


def window(padded, axis, offset, start, count):
    begin = list(start)
    begin[axis] = begin[axis] + offset
    return lax.slice(padded, begin, [b + c for b, c in zip(begin, count)])


def forward_diff(padded, axis, start, count):
    total = 0.0
    for order, coef in enumerate(COEFS, 1):
        total = total + coef * (window(padded, axis, order, start, count) - window(padded, axis, 1 - order, start, count))
    return total


def backward_diff(padded, axis, start, count):
    total = 0.0
    for order, coef in enumerate(COEFS, 1):
        total = total + coef * (window(padded, axis, order - 1, start, count) - window(padded, axis, -order, start, count))
    return total


def divergence(stress, start, count):
    sxx, syy, szz, sxy, sxz, syz = stress
    force_x = forward_diff(sxx, 0, start, count) + backward_diff(sxy, 1, start, count) + backward_diff(sxz, 2, start, count)
    force_y = backward_diff(sxy, 0, start, count) + forward_diff(syy, 1, start, count) + backward_diff(syz, 2, start, count)
    force_z = backward_diff(sxz, 0, start, count) + backward_diff(syz, 1, start, count) + forward_diff(szz, 2, start, count)
    return (force_x, force_y, force_z)


def strain(velocity, start, count):
    vel_x, vel_y, vel_z = velocity
    exx = backward_diff(vel_x, 0, start, count)
    eyy = backward_diff(vel_y, 1, start, count)
    ezz = backward_diff(vel_z, 2, start, count)
    exy = forward_diff(vel_x, 1, start, count) + forward_diff(vel_y, 0, start, count)
    exz = forward_diff(vel_x, 2, start, count) + forward_diff(vel_z, 0, start, count)
    eyz = forward_diff(vel_y, 2, start, count) + forward_diff(vel_z, 1, start, count)
    return (exx, eyy, ezz, exy, exz, eyz)


def update_stress(stress, rates, lame_lambda, lame_mu, damp):
    trace = rates[0] + rates[1] + rates[2]
    result = []
    for k in range(3):
        result.append(damp * (stress[k] + TIME_STEP * (lame_lambda * trace + 2.0 * lame_mu * rates[k])))
    for k in range(3, 6):
        result.append(damp * (stress[k] + TIME_STEP * lame_mu * rates[k]))
    return result


def taper(dist, width):
    frac = jnp.maximum(width - dist.astype(jnp.float32), 0.0) / width
    return jnp.exp(-DAMPING * frac * frac)


def imaging(grads, rates, adjoint, vel_after, vel_before):
    exx, eyy, ezz, exy, exz, eyz = rates
    g_lambda = grads[0] + (exx + eyy + ezz) * (adjoint[3] + adjoint[4] + adjoint[5])
    g_mu = grads[1] + 2.0 * (exx * adjoint[3] + eyy * adjoint[4] + ezz * adjoint[5]) + exy * adjoint[6] + exz * adjoint[7] + eyz * adjoint[8]
    g_rho = grads[2] + (adjoint[0] * (vel_after[0] - vel_before[0]) + adjoint[1] * (vel_after[1] - vel_before[1]) + adjoint[2] * (vel_after[2] - vel_before[2])) / TIME_STEP
    return (g_lambda, g_mu, g_rho)


def reference(forward_state, adjoint_state, lame_lambda, lame_mu, buoyancy, source_x, source_y, source_z, source_wavelet, receiver_x, receiver_y, receiver_residual, absorb_width):
    start = (4, 4, 4)
    count = (NX, NY, NZ)
    width = absorb_width[0].astype(jnp.float32)
    coord_x = jnp.arange(NX, dtype=jnp.int32)
    coord_y = jnp.arange(NY, dtype=jnp.int32)
    coord_z = jnp.arange(NZ, dtype=jnp.int32)
    taper_x = taper(jnp.minimum(coord_x, NX - 1 - coord_x), width)
    taper_y = taper(jnp.minimum(coord_y, NY - 1 - coord_y), width)
    taper_z = taper(NZ - 1 - coord_z, width)
    damp = taper_x[:, None, None] * taper_y[None, :, None] * taper_z[None, None, :]

    def velocity_half(state):
        stress = tuple(jnp.pad(state[k], 4) for k in range(3, 9))
        force = divergence(stress, start, count)
        return [damp * (state[k] + TIME_STEP * buoyancy * force[k]) for k in range(3)]

    def full_step(state):
        velocity = velocity_half(state)
        rates = strain(tuple(jnp.pad(v, 4) for v in velocity), start, count)
        stress = update_stress([state[k] for k in range(3, 9)], rates, lame_lambda, lame_mu, damp)
        return rates, velocity, stress

    rates_one, vel_one, stress_one = full_step(forward_state)
    for k in range(3):
        stress_one[k] = stress_one[k].at[source_x, source_y, source_z].add(TIME_STEP * source_wavelet)
    state_one = jnp.stack(vel_one + stress_one)
    vel_two = velocity_half(state_one)
    rates_two = strain(tuple(jnp.pad(v, 4) for v in vel_two), start, count)

    depth_cells = jnp.full_like(receiver_x, REC_DEPTH)
    unused_rates, adj_vel, adj_stress = full_step(adjoint_state)
    adj_vel[2] = adj_vel[2].at[receiver_x, receiver_y, depth_cells].add(TIME_STEP * receiver_residual[0])
    adjoint_one = jnp.stack(adj_vel + adj_stress)
    unused_rates, adj_vel, adj_stress = full_step(adjoint_one)
    adj_vel[2] = adj_vel[2].at[receiver_x, receiver_y, depth_cells].add(TIME_STEP * receiver_residual[1])
    adjoint_zero = jnp.stack(adj_vel + adj_stress)

    zero = jnp.zeros((NX, NY, NZ), jnp.float32)
    grads = (zero, zero, zero)
    grads = imaging(grads, rates_two, adjoint_one, vel_two, vel_one)
    grads = imaging(grads, rates_one, adjoint_zero, vel_one, [forward_state[k] for k in range(3)])
    return grads[0], grads[1], grads[2]
```

```python
import jax
import jax.numpy as jnp
from jax import lax
from jax.experimental import pallas as pl
from jax.experimental.pallas import tpu as pltpu
from jax.sharding import PartitionSpec as P

REC_DEPTH = 6
COEFS = (1225.0 / 1024.0, -245.0 / 3072.0, 49.0 / 5120.0, -5.0 / 7168.0)
TIME_STEP = 0.2
DAMPING = 0.3
MESH = pl.DeviceIdType.MESH

FS0, FV1, FS1, FV2, AS0, AV1, AS1, AV0 = range(8)
VELOCITY = (FV1, FV2, AV1, AV0)
UP, DOWN = 0, 1


def layers(e, way, c):
    backward = (c == 0) if e in VELOCITY else (c != 0)
    return 4 if backward == (way == UP) else 3


def diff(load, forward):
    total = None
    for order, coef in enumerate(COEFS, 1):
        high, low = (order, 1 - order) if forward else (order - 1, -order)
        term = coef * (load(high) - load(low))
        total = term if total is None else total + term
    return total


def kernel(
    fwd, adj, lam_in, mu_in, buo_in, src_x, src_y, src_z, src_w, width_in, rec_x, rec_y, residual,
    g_lam, g_mu, g_rho,
    px, py, ys, yr, szz, vel0, lam, mu, buo, damp, src, rinj, rates1,
    load_sem, xs_sem, xr_sem, ys_sem, yr_sem,
):
    gx, gy = lax.axis_index("gx"), lax.axis_index("gy")
    nx, ny = lax.axis_size("gx"), lax.axis_size("gy")
    cells_x, cells_y, depth = buo.shape
    pairs = cells_x // 2
    anchor_x, anchor_y = gx * cells_x, gy * cells_y
    total_x, total_y = nx * cells_x, ny * cells_y
    has = {("gx", UP): gx < nx - 1, ("gx", DOWN): gx > 0, ("gy", UP): gy < ny - 1, ("gy", DOWN): gy > 0}
    place = {"gx": gx, "gy": gy}

    def neighbour(axis, way):
        return {axis: place[axis] + (1 if way == UP else -1)}

    loads = {}

    def load(name, source, target):
        copy = pltpu.make_async_copy(source, target, load_sem.at[len(loads)])
        copy.start()
        loads[name] = copy

    middle, rows = pl.ds(4, cells_x), pl.ds(8, cells_y)
    for chain, (state, e) in enumerate(((fwd, FS0), (adj, AS0))):
        for c, k in enumerate((3, 6, 7)):
            load(("px", e, c), state.at[k], px.at[e, c, middle])
        for c, k in enumerate((4, 6, 8)):
            load(("py", e, c), state.at[k], py.at[e, c, :, rows])
    for chain, (state, e) in enumerate(((fwd, FS0), (adj, AS0))):
        load(("szz", e), state.at[5], szz.at[e])
        load(("vel", e), state.at[pl.ds(0, 3)], vel0.at[chain])
    load("buo", buo_in, buo)
    load("lam", lam_in, lam)
    load("mu", mu_in, mu)

    barrier = pltpu.get_barrier_semaphore()
    for (axis, way), there in has.items():
        @pl.when(there)
        def _(axis=axis, way=way):
            pl.semaphore_signal(barrier, inc=1, device_id=neighbour(axis, way), device_id_type=MESH)

    row = lax.broadcasted_iota(jnp.int32, (cells_y, depth), 0)
    lane = lax.broadcasted_iota(jnp.int32, (cells_y, depth), 1)
    width = width_in[0].astype(jnp.float32)

    def taper(dist):
        frac = jnp.maximum(width - dist.astype(jnp.float32), 0.0) / width
        return jnp.exp(-DAMPING * frac * frac)

    coord_y = anchor_y + row
    taper_y = taper(jnp.minimum(coord_y, total_y - 1 - coord_y))
    taper_z = taper(depth - 1 - lane)
    rec_row = anchor_y + lax.broadcasted_iota(jnp.int32, (cells_y, rec_x.shape[1]), 0) == rec_y[...]

    def prepare(p, carry):
        coord_x = jnp.zeros((cells_y, depth), jnp.int32) + (anchor_x + p)
        damp[p] = taper(jnp.minimum(coord_x, total_x - 1 - coord_x)) * taper_y * taper_z
        total = jnp.zeros((cells_y, depth), jnp.float32)
        for s in range(src_x.shape[0]):
            amount = jnp.where(src_x[s] == anchor_x + p, TIME_STEP * src_w[s], 0.0)
            hit = (coord_y == src_y[s]) & (lane == src_z[s])
            total = total + jnp.where(hit, amount, 0.0)
        src[p] = total
        for t in range(2):
            amounts = jnp.where(rec_x[...] == anchor_x + p, TIME_STEP * residual[pl.ds(t, 1), :], 0.0)
            column = jnp.sum(jnp.where(rec_row, amounts, 0.0), axis=1, keepdims=True)
            rinj[t, p] = jnp.where(lane == REC_DEPTH, column, 0.0)
        return carry

    lax.fori_loop(0, cells_x, prepare, 0)

    for way in (UP, DOWN):
        @pl.when(jnp.logical_not(has["gx", 1 - way]))
        def _(way=way):
            def fill(e, carry):
                px[e, :, pl.ds(0 if way == UP else 4 + cells_x, 4)] = jnp.zeros((3, 4, cells_y, depth), jnp.float32)
                return carry
            lax.fori_loop(0, 8, fill, 0)

        @pl.when(jnp.logical_not(has["gy", 1 - way]))
        def _(way=way):
            def fill(e, carry):
                yr[e, way] = jnp.zeros(yr.shape[2:], jnp.float32)
                return carry
            lax.fori_loop(0, 8, fill, 0)

    def x_copy(e, way, c, peer):
        n = layers(e, way, c)
        if way == UP:
            source, target = pl.ds(4 + cells_x - n, n), pl.ds(4 - n, n)
        else:
            source, target = pl.ds(4, n), pl.ds(4 + cells_x, n)
        return pltpu.make_async_remote_copy(
            px.at[e, c, source], px.at[e, c, target], xs_sem.at[e, way, c], xr_sem.at[e, way, c],
            device_id=neighbour("gx", peer), device_id_type=MESH,
        )

    def y_copy(e, way, peer):
        return pltpu.make_async_remote_copy(
            ys.at[e, way], yr.at[e, way], ys_sem.at[e, way], yr_sem.at[e, way],
            device_id=neighbour("gy", peer), device_id_type=MESH,
        )

    def send(e):
        for way in (UP, DOWN):
            @pl.when(has["gx", way])
            def _(way=way):
                for c in range(3):
                    x_copy(e, way, c, way).start()
        for way in (UP, DOWN):
            @pl.when(has["gy", way])
            def _(way=way):
                y_copy(e, way, way).start()

    def slot(c, p, odd):
        if c < 2:
            return p, pl.ds(4 * c, 4)
        return cells_x + p // 2, pl.ds(4 * odd, 4)

    def receive(e):
        for way in (UP, DOWN):
            @pl.when(has["gy", 1 - way])
            def _(way=way):
                y_copy(e, way, 1 - way).wait_recv()

        def unpack(q, carry):
            for odd in range(2):
                p = 2 * q + odd
                for c in range(3):
                    tile, part = slot(c, p, odd) if c < 2 else (cells_x + q, pl.ds(4 * odd, 4))
                    py[e, c, p, pl.ds(4, 4), :] = yr[e, UP, tile, part, :]
                    py[e, c, p, pl.ds(8 + cells_y, 4), :] = yr[e, DOWN, tile, part, :]
            return carry

        lax.fori_loop(0, pairs, unpack, 0)
        for way in (UP, DOWN):
            @pl.when(has["gx", 1 - way])
            def _(way=way):
                for c in range(3):
                    x_copy(e, way, c, 1 - way).wait_recv()

    def pack(e, c, q, odd, value):
        tile, part = (2 * q + odd, pl.ds(4 * c, 4)) if c < 2 else (cells_x + q, pl.ds(4 * odd, 4))
        ys[e, UP, tile, part, :] = value[cells_y - 4:]
        ys[e, DOWN, tile, part, :] = value[:4]

    def store_y(e, c, q, odd, value):
        py[e, c, 2 * q + odd, rows, :] = value
        pack(e, c, q, odd, value)

    def by_plane(body):
        def step(q, carry):
            for odd in range(2):
                body(q, odd, 2 * q + odd)
            return carry
        lax.fori_loop(0, pairs, step, 0)

    def diff_x(e, c, p, forward):
        return diff(lambda k: px[e, c, p + (4 + k)], forward)

    def diff_y(e, c, p, forward):
        return diff(lambda k: py[e, c, p, pl.ds(8 + k, cells_y), :], forward)

    def diff_z(value, forward):
        def at(k):
            if k == 0:
                return value
            moved = pltpu.roll(value, (-k) % depth, 1)
            return jnp.where(lane < depth - k if k > 0 else lane >= -k, moved, 0.0)
        return diff(at, forward)

    def center_x(e, c, p):
        return px[e, c, p + 4]

    def center_y(e, c, p):
        return py[e, c, p, rows, :]

    def stresses(e, p):
        return (
            center_x(e, 0, p), center_y(e, 0, p), szz[e, p],
            center_x(e, 1, p), center_x(e, 2, p), center_y(e, 2, p),
        )

    def velocity_half(e, target, before):
        def body(q, odd, p):
            s = stresses(e, p)
            force = (
                diff_x(e, 0, p, True) + diff_y(e, 1, p, False) + diff_z(s[4], False),
                diff_x(e, 1, p, False) + diff_y(e, 0, p, True) + diff_z(s[5], False),
                diff_x(e, 2, p, False) + diff_y(e, 2, p, False) + diff_z(s[2], True),
            )
            scaled = TIME_STEP * buo[p]
            for c in range(3):
                value = damp[p] * (before(c, p) + scaled * force[c])
                px[target, c, p + 4] = value
                store_y(target, c, q, odd, value)
        by_plane(body)

    def strain(e, p):
        vx, vy, vz = (center_x(e, c, p) for c in range(3))
        return (
            diff_x(e, 0, p, False),
            diff_y(e, 1, p, False),
            diff_z(vz, False),
            diff_y(e, 0, p, True) + diff_x(e, 1, p, True),
            diff_z(vx, True) + diff_x(e, 2, p, True),
            diff_z(vy, True) + diff_y(e, 2, p, True),
        )

    def stress_half(e, rates, p):
        s = stresses(e, p)
        normal = lam[p] * (rates[0] + rates[1] + rates[2])
        shear = TIME_STEP * mu[p]
        return [
            damp[p] * (s[k] + (TIME_STEP * normal + 2.0 * shear * rates[k])) for k in range(3)
        ] + [damp[p] * (s[k] + shear * rates[k]) for k in range(3, 6)]

    def store_stress(e, q, odd, p, s):
        for c, k in enumerate((0, 3, 4)):
            px[e, c, p + 4] = s[k]
        for c, k in enumerate((1, 3, 5)):
            store_y(e, c, q, odd, s[k])
        szz[e, p] = s[2]

    for e in (FS0, AS0):
        for c in range(3):
            loads["py", e, c].wait()

        def first(q, odd, p, e=e):
            for c in range(3):
                pack(e, c, q, odd, center_y(e, c, p))
        by_plane(first)
        for c in range(3):
            loads["px", e, c].wait()

    pl.semaphore_wait(barrier, sum(there.astype(jnp.int32) for there in has.values()))

    send(FS0)
    send(AS0)
    for name, copy in loads.items():
        if name[0] not in ("px", "py"):
            copy.wait()

    receive(FS0)
    velocity_half(FS0, FV1, lambda c, p: vel0[0, c, p])
    send(FV1)
    receive(AS0)
    velocity_half(AS0, AV1, lambda c, p: vel0[1, c, p])
    send(AV1)

    receive(FV1)

    def forward_stress(q, odd, p):
        rates = strain(FV1, p)
        for k in range(6):
            rates1[k, p] = rates[k]
        s = stress_half(FS0, rates, p)
        for k in range(3):
            s[k] = s[k] + src[p]
        store_stress(FS1, q, odd, p, s)
    by_plane(forward_stress)
    send(FS1)

    receive(AV1)

    def adjoint_stress(q, odd, p):
        store_stress(AS1, q, odd, p, stress_half(AS0, strain(AV1, p), p))
    by_plane(adjoint_stress)
    send(AS1)

    receive(FS1)
    velocity_half(FS1, FV2, lambda c, p: center_x(FV1, c, p))
    send(FV2)

    def adjoint_velocity(e, t, c, p):
        value = center_x(e, c, p)
        return value + rinj[t, p] if c == 2 else value

    receive(AS1)
    velocity_half(AS1, AV0, lambda c, p: adjoint_velocity(AV1, 0, c, p))
    send(AV0)

    def density(q, odd, p):
        total = None
        for c in range(3):
            one = center_x(FV1, c, p)
            term = (
                adjoint_velocity(AV1, 0, c, p) * (center_x(FV2, c, p) - one)
                + adjoint_velocity(AV0, 1, c, p) * (one - vel0[0, c, p])
            )
            total = term if total is None else total + term
        g_rho[p] = total / TIME_STEP
    by_plane(density)

    def image(rates, s):
        lam_term = (rates[0] + rates[1] + rates[2]) * (s[0] + s[1] + s[2])
        normal = rates[0] * s[0] + rates[1] * s[1] + rates[2] * s[2]
        return lam_term, 2.0 * normal + rates[3] * s[3] + rates[4] * s[4] + rates[5] * s[5]

    receive(FV2)

    def image_one(q, odd, p):
        g_lam[p], g_mu[p] = image(strain(FV2, p), stresses(AS1, p))
    by_plane(image_one)

    receive(AV0)

    def image_two(q, odd, p):
        s = stress_half(AS1, strain(AV0, p), p)
        lam_term, mu_term = image([rates1[k, p] for k in range(6)], s)
        g_lam[p] = g_lam[p] + lam_term
        g_mu[p] = g_mu[p] + mu_term
    by_plane(image_two)

    for e in range(8):
        for way in (UP, DOWN):
            @pl.when(has["gx", way])
            def _(e=e, way=way):
                for c in range(3):
                    x_copy(e, way, c, way).wait_send()

            @pl.when(has["gy", way])
            def _(e=e, way=way):
                y_copy(e, way, way).wait_send()


def local(
    forward_state, adjoint_state, lame_lambda, lame_mu, buoyancy,
    source_x, source_y, source_z, source_wavelet,
    receiver_x, receiver_y, receiver_residual, absorb_width,
):
    block = buoyancy.shape
    cells_x, cells_y, depth = block
    f32 = jnp.float32
    hbm, vmem, smem = (pl.BlockSpec(memory_space=m) for m in (pl.ANY, pltpu.VMEM, pltpu.SMEM))
    dma = pltpu.SemaphoreType.DMA
    packed = (8, 2, cells_x + cells_x // 2, 8, depth)
    return pl.pallas_call(
        kernel,
        out_shape=[jax.ShapeDtypeStruct(block, f32)] * 3,
        in_specs=[hbm] * 5 + [smem] * 5 + [vmem] * 3,
        out_specs=[vmem] * 3,
        scratch_shapes=[
            pltpu.VMEM((8, 3, cells_x + 8, cells_y, depth), f32),
            pltpu.VMEM((8, 3, cells_x, cells_y + 16, depth), f32),
            pltpu.VMEM(packed, f32),
            pltpu.VMEM(packed, f32),
            pltpu.VMEM((8,) + block, f32),
            pltpu.VMEM((2, 3) + block, f32),
            pltpu.VMEM(block, f32),
            pltpu.VMEM(block, f32),
            pltpu.VMEM(block, f32),
            pltpu.VMEM(block, f32),
            pltpu.VMEM(block, f32),
            pltpu.VMEM((2,) + block, f32),
            pltpu.VMEM((6,) + block, f32),
            dma((19,)),
            dma((8, 2, 3)),
            dma((8, 2, 3)),
            dma((8, 2)),
            dma((8, 2)),
        ],
        compiler_params=pltpu.CompilerParams(
            collective_id=0, has_side_effects=True, vmem_limit_bytes=60 * 1024 * 1024
        ),
        name="window",
    )(
        forward_state, adjoint_state, lame_lambda, lame_mu, buoyancy,
        source_x, source_y, source_z, source_wavelet, absorb_width,
        receiver_x.reshape(1, -1), receiver_y.reshape(1, -1), receiver_residual,
    )


def solution(mesh):
    volume = P("gx", "gy", None)
    state = P(None, "gx", "gy", None)
    return jax.shard_map(
        local,
        mesh=mesh,
        in_specs=(state, state, volume, volume, volume) + (P(),) * 8,
        out_specs=(volume, volume, volume),
        check_vma=False,
    )
```

```python
import jax
import jax.numpy as jnp
from jax import lax
from jax.experimental import pallas as pl
from jax.experimental.pallas import tpu as pltpu
from jax.sharding import PartitionSpec as P

REC_DEPTH = 6
COEFS = (1225.0 / 1024.0, -245.0 / 3072.0, 49.0 / 5120.0, -5.0 / 7168.0)
TIME_STEP = 0.2
DAMPING = 0.3
MESH = pl.DeviceIdType.MESH

FS0, FV1, FS1, FV2, AS0, AV1, AS1, AV0 = range(8)
VELOCITY = (FV1, FV2, AV1, AV0)
UP, DOWN = 0, 1


def layers(e, way, c):
    backward = (c == 0) if e in VELOCITY else (c != 0)
    return 4 if backward == (way == UP) else 3


def diff(load, forward):
    total = None
    for order, coef in enumerate(COEFS, 1):
        high, low = (order, 1 - order) if forward else (order - 1, -order)
        term = coef * (load(high) - load(low))
        total = term if total is None else total + term
    return total


def kernel(
    fwd, adj, lam_in, mu_in, buo_in, src_x, src_y, src_z, src_w, width_in, rec_x, rec_y, residual,
    g_lam, g_mu, g_rho,
    px, py, ys, yr, szz, vel0, lam, mu, buo, damp, src, rinj, rates1,
    load_sem, xs_sem, xr_sem, ys_sem, yr_sem,
):
    gx, gy = lax.axis_index("gx"), lax.axis_index("gy")
    nx, ny = lax.axis_size("gx"), lax.axis_size("gy")
    cells_x, cells_y, depth = buo.shape
    pairs = cells_x // 2
    anchor_x, anchor_y = gx * cells_x, gy * cells_y
    total_x, total_y = nx * cells_x, ny * cells_y
    has = {("gx", UP): gx < nx - 1, ("gx", DOWN): gx > 0, ("gy", UP): gy < ny - 1, ("gy", DOWN): gy > 0}
    place = {"gx": gx, "gy": gy}

    def neighbour(axis, way):
        return {axis: place[axis] + (1 if way == UP else -1)}

    loads = {}

    def load(name, source, target):
        copy = pltpu.make_async_copy(source, target, load_sem.at[len(loads)])
        copy.start()
        loads[name] = copy

    middle, rows = pl.ds(4, cells_x), pl.ds(8, cells_y)
    for chain, (state, e) in enumerate(((fwd, FS0), (adj, AS0))):
        for c, k in enumerate((3, 6, 7)):
            load(("px", e, c), state.at[k], px.at[e, c, middle])
        for c, k in enumerate((4, 6, 8)):
            load(("py", e, c), state.at[k], py.at[e, c, :, rows])
    for chain, (state, e) in enumerate(((fwd, FS0), (adj, AS0))):
        load(("szz", e), state.at[5], szz.at[e])
        load(("vel", e), state.at[pl.ds(0, 3)], vel0.at[chain])
    load("buo", buo_in, buo)
    load("lam", lam_in, lam)
    load("mu", mu_in, mu)

    barrier = pltpu.get_barrier_semaphore()
    for (axis, way), there in has.items():
        @pl.when(there)
        def _(axis=axis, way=way):
            pl.semaphore_signal(barrier, inc=1, device_id=neighbour(axis, way), device_id_type=MESH)

    row = lax.broadcasted_iota(jnp.int32, (cells_y, depth), 0)
    lane = lax.broadcasted_iota(jnp.int32, (cells_y, depth), 1)
    coord_y = anchor_y + row

    def set_damping():
        width = width_in[0].astype(jnp.float32)

        def taper(dist):
            frac = jnp.maximum(width - dist.astype(jnp.float32), 0.0) / width
            return jnp.exp(-DAMPING * frac * frac)

        taper_y = taper(jnp.minimum(coord_y, total_y - 1 - coord_y))
        taper_z = taper(depth - 1 - lane)

        def plane(p, carry):
            coord_x = jnp.zeros((cells_y, depth), jnp.int32) + (anchor_x + p)
            damp[p] = taper(jnp.minimum(coord_x, total_x - 1 - coord_x)) * taper_y * taper_z
            return carry

        lax.fori_loop(0, cells_x, plane, 0)

    def set_injections():
        rec_row = anchor_y + lax.broadcasted_iota(jnp.int32, (cells_y, rec_x.shape[1]), 0) == rec_y[...]

        def plane(p, carry):
            total = jnp.zeros((cells_y, depth), jnp.float32)
            for s in range(src_x.shape[0]):
                amount = jnp.where(src_x[s] == anchor_x + p, TIME_STEP * src_w[s], 0.0)
                hit = (coord_y == src_y[s]) & (lane == src_z[s])
                total = total + jnp.where(hit, amount, 0.0)
            src[p] = total
            for t in range(2):
                amounts = jnp.where(rec_x[...] == anchor_x + p, TIME_STEP * residual[pl.ds(t, 1), :], 0.0)
                column = jnp.sum(jnp.where(rec_row, amounts, 0.0), axis=1, keepdims=True)
                rinj[t, p] = jnp.where(lane == REC_DEPTH, column, 0.0)
            return carry

        lax.fori_loop(0, cells_x, plane, 0)

    def set_zeros():
        for way in (UP, DOWN):
            @pl.when(jnp.logical_not(has["gx", 1 - way]))
            def _(way=way):
                def fill(e, carry):
                    px[e, :, pl.ds(0 if way == UP else 4 + cells_x, 4)] = jnp.zeros((3, 4, cells_y, depth), jnp.float32)
                    return carry
                lax.fori_loop(0, 8, fill, 0)

            @pl.when(jnp.logical_not(has["gy", 1 - way]))
            def _(way=way):
                def fill(e, carry):
                    yr[e, way] = jnp.zeros(yr.shape[2:], jnp.float32)
                    return carry
                lax.fori_loop(0, 8, fill, 0)

    def x_copy(e, way, c, peer):
        n = layers(e, way, c)
        if way == UP:
            source, target = pl.ds(4 + cells_x - n, n), pl.ds(4 - n, n)
        else:
            source, target = pl.ds(4, n), pl.ds(4 + cells_x, n)
        return pltpu.make_async_remote_copy(
            px.at[e, c, source], px.at[e, c, target], xs_sem.at[e, way, c], xr_sem.at[e, way, c],
            device_id=neighbour("gx", peer), device_id_type=MESH,
        )

    def y_copy(e, way, peer):
        return pltpu.make_async_remote_copy(
            ys.at[e, way], yr.at[e, way], ys_sem.at[e, way], yr_sem.at[e, way],
            device_id=neighbour("gy", peer), device_id_type=MESH,
        )

    odd_block = lax.rem(gx, 2)
    is_near = {UP: odd_block == 0, DOWN: odd_block == 1}

    def x_side(near, way):
        there = is_near[way] if near else jnp.logical_not(is_near[way])
        return jnp.logical_and(there, has["gx", way])

    def send_x(e, near):
        for way in (UP, DOWN):
            @pl.when(x_side(near, way))
            def _(way=way):
                for c in range(3):
                    x_copy(e, way, c, way).start()

    def sent_x(e, near):
        for way in (UP, DOWN):
            @pl.when(x_side(near, way))
            def _(way=way):
                for c in range(3):
                    x_copy(e, way, c, way).wait_send()

    def receive_x(e, near):
        for way in (UP, DOWN):
            @pl.when(x_side(near, 1 - way))
            def _(way=way):
                for c in range(3):
                    x_copy(e, way, c, 1 - way).wait_recv()

    def send_y(e):
        for way in (UP, DOWN):
            @pl.when(has["gy", way])
            def _(way=way):
                y_copy(e, way, way).start()

    def sent_y(e):
        for way in (UP, DOWN):
            @pl.when(has["gy", way])
            def _(way=way):
                y_copy(e, way, way).wait_send()

    def receive_y(e):
        for way in (UP, DOWN):
            @pl.when(has["gy", 1 - way])
            def _(way=way):
                y_copy(e, way, 1 - way).wait_recv()

        def unpack(q, odd, p):
            for c in range(3):
                tile, part = slot(c, q, odd)
                py[e, c, p, pl.ds(4, 4), :] = yr[e, UP, tile, part, :]
                py[e, c, p, pl.ds(8 + cells_y, 4), :] = yr[e, DOWN, tile, part, :]
        by_plane(unpack)

    def slot(c, q, odd):
        if c < 2:
            return 2 * q + odd, pl.ds(4 * c, 4)
        return cells_x + q, pl.ds(4 * odd, 4)

    def pack(e, c, q, odd, value):
        tile, part = slot(c, q, odd)
        ys[e, UP, tile, part, :] = value[cells_y - 4:]
        ys[e, DOWN, tile, part, :] = value[:4]

    def store_y(e, c, q, odd, value):
        py[e, c, 2 * q + odd, rows, :] = value
        pack(e, c, q, odd, value)

    def by_plane(body, first=0, count=pairs):
        def step(i, carry):
            q = first + i
            for odd in range(2):
                body(q, odd, 2 * q + odd)
            return carry
        lax.fori_loop(0, count, step, 0)

    half = pairs // 2
    first_pair = {True: half * (1 - odd_block), False: half * odd_block}

    def near_half(e, body, target=None):
        receive_y(e)
        receive_x(e, True)
        by_plane(body, first_pair[True], half)
        if target is not None:
            send_x(target, True)

    def far_half(e, body, target=None):
        receive_x(e, False)
        by_plane(body, first_pair[False], half)
        if target is not None:
            send_x(target, False)
            send_y(target)

    def diff_x(e, c, p, forward):
        return diff(lambda k: px[e, c, p + (4 + k)], forward)

    def diff_y(e, c, p, forward):
        return diff(lambda k: py[e, c, p, pl.ds(8 + k, cells_y), :], forward)

    def diff_z(value, forward):
        def at(k):
            if k == 0:
                return value
            moved = pltpu.roll(value, (-k) % depth, 1)
            return jnp.where(lane < depth - k if k > 0 else lane >= -k, moved, 0.0)
        return diff(at, forward)

    def center_x(e, c, p):
        return px[e, c, p + 4]

    def center_y(e, c, p):
        return py[e, c, p, rows, :]

    def stresses(e, p):
        return (
            center_x(e, 0, p), center_y(e, 0, p), szz[e, p],
            center_x(e, 1, p), center_x(e, 2, p), center_y(e, 2, p),
        )

    def velocity_half(e, target, before):
        def body(q, odd, p):
            s = stresses(e, p)
            force = (
                diff_x(e, 0, p, True) + diff_y(e, 1, p, False) + diff_z(s[4], False),
                diff_x(e, 1, p, False) + diff_y(e, 0, p, True) + diff_z(s[5], False),
                diff_x(e, 2, p, False) + diff_y(e, 2, p, False) + diff_z(s[2], True),
            )
            scaled = TIME_STEP * buo[p]
            for c in range(3):
                value = damp[p] * (before(c, p) + scaled * force[c])
                px[target, c, p + 4] = value
                store_y(target, c, q, odd, value)
        return body

    def strain(e, p):
        vx, vy, vz = (center_x(e, c, p) for c in range(3))
        return (
            diff_x(e, 0, p, False),
            diff_y(e, 1, p, False),
            diff_z(vz, False),
            diff_y(e, 0, p, True) + diff_x(e, 1, p, True),
            diff_z(vx, True) + diff_x(e, 2, p, True),
            diff_z(vy, True) + diff_y(e, 2, p, True),
        )

    def stress_half(e, rates, p):
        s = stresses(e, p)
        normal = lam[p] * (rates[0] + rates[1] + rates[2])
        shear = TIME_STEP * mu[p]
        return [
            damp[p] * (s[k] + (TIME_STEP * normal + 2.0 * shear * rates[k])) for k in range(3)
        ] + [damp[p] * (s[k] + shear * rates[k]) for k in range(3, 6)]

    def store_stress(e, q, odd, p, s):
        for c, k in enumerate((0, 3, 4)):
            px[e, c, p + 4] = s[k]
        for c, k in enumerate((1, 3, 5)):
            store_y(e, c, q, odd, s[k])
        szz[e, p] = s[2]

    def forward_stress(q, odd, p):
        rates = strain(FV1, p)
        for k in range(6):
            rates1[k, p] = rates[k]
        s = stress_half(FS0, rates, p)
        for k in range(3):
            s[k] = s[k] + src[p]
        store_stress(FS1, q, odd, p, s)

    def adjoint_stress(q, odd, p):
        store_stress(AS1, q, odd, p, stress_half(AS0, strain(AV1, p), p))

    def adjoint_velocity(e, t, c, p):
        value = center_x(e, c, p)
        return value + rinj[t, p] if c == 2 else value

    def density(q, odd, p):
        total = None
        for c in range(3):
            one = center_x(FV1, c, p)
            term = (
                adjoint_velocity(AV1, 0, c, p) * (center_x(FV2, c, p) - one)
                + adjoint_velocity(AV0, 1, c, p) * (one - vel0[0, c, p])
            )
            total = term if total is None else total + term
        g_rho[p] = total / TIME_STEP

    def image(rates, s):
        lam_term = (rates[0] + rates[1] + rates[2]) * (s[0] + s[1] + s[2])
        normal = rates[0] * s[0] + rates[1] * s[1] + rates[2] * s[2]
        return lam_term, 2.0 * normal + rates[3] * s[3] + rates[4] * s[4] + rates[5] * s[5]

    def image_one(q, odd, p):
        g_lam[p], g_mu[p] = image(strain(FV2, p), stresses(AS1, p))

    def image_two(q, odd, p):
        s = stress_half(AS1, strain(AV0, p), p)
        lam_term, mu_term = image([rates1[k, p] for k in range(6)], s)
        g_lam[p] = g_lam[p] + lam_term
        g_mu[p] = g_mu[p] + mu_term

    forward_one = velocity_half(FS0, FV1, lambda c, p: vel0[0, c, p])
    adjoint_one = velocity_half(AS0, AV1, lambda c, p: vel0[1, c, p])
    forward_two = velocity_half(FS1, FV2, lambda c, p: center_x(FV1, c, p))
    adjoint_two = velocity_half(AS1, AV0, lambda c, p: adjoint_velocity(AV1, 0, c, p))

    def ready(e):
        for c in range(3):
            loads["py", e, c].wait()

        def first(q, odd, p):
            for c in range(3):
                pack(e, c, q, odd, center_y(e, c, p))
        by_plane(first)
        for c in range(3):
            loads["px", e, c].wait()

    ready(FS0)
    ready(AS0)
    set_damping()
    pl.semaphore_wait(barrier, sum(there.astype(jnp.int32) for there in has.values()))
    for near in (False, True):
        send_x(FS0, near)
    send_y(FS0)
    set_zeros()
    set_injections()
    for name, copy in loads.items():
        if name[0] not in ("px", "py"):
            copy.wait()

    near_half(FS0, forward_one, FV1)
    sent_x(FS0, False)
    for near in (False, True):
        send_x(AS0, near)
    send_y(AS0)
    near_half(AS0, adjoint_one, AV1)

    far_half(FS0, forward_one, FV1)
    near_half(FV1, forward_stress, FS1)
    far_half(AS0, adjoint_one, AV1)
    near_half(AV1, adjoint_stress, AS1)

    far_half(FV1, forward_stress, FS1)
    near_half(FS1, forward_two, FV2)
    far_half(AV1, adjoint_stress, AS1)
    near_half(AS1, adjoint_two, AV0)

    far_half(FS1, forward_two, FV2)
    near_half(FV2, image_one)
    far_half(AS1, adjoint_two, AV0)
    by_plane(density)
    near_half(AV0, image_two)

    far_half(FV2, image_one)
    far_half(AV0, image_two)

    for e in range(8):
        if e != FS0:
            sent_x(e, False)
        sent_x(e, True)
        sent_y(e)


def hand_on(*refs):
    count = len(refs) // 2
    sem = refs[-1]
    copies = [pltpu.make_async_copy(refs[i], refs[count + i], sem.at[i]) for i in range(count)]
    for copy in copies:
        copy.start()
    for copy in copies:
        copy.wait()


def local(
    forward_state, adjoint_state, lame_lambda, lame_mu, buoyancy,
    source_x, source_y, source_z, source_wavelet,
    receiver_x, receiver_y, receiver_residual, absorb_width,
):
    block = buoyancy.shape
    cells_x, cells_y, depth = block
    f32 = jnp.float32
    hbm, vmem, smem = (pl.BlockSpec(memory_space=m) for m in (pl.ANY, pltpu.VMEM, pltpu.SMEM))
    dma = pltpu.SemaphoreType.DMA
    packed = (8, 2, cells_x + cells_x // 2, 8, depth)
    shapes = [jax.ShapeDtypeStruct(block, f32)] * 3
    grads = pl.pallas_call(
        kernel,
        out_shape=shapes,
        in_specs=[hbm] * 5 + [smem] * 5 + [vmem] * 3,
        out_specs=[vmem] * 3,
        scratch_shapes=[
            pltpu.VMEM((8, 3, cells_x + 8, cells_y, depth), f32),
            pltpu.VMEM((8, 3, cells_x, cells_y + 16, depth), f32),
            pltpu.VMEM(packed, f32),
            pltpu.VMEM(packed, f32),
            pltpu.VMEM((8,) + block, f32),
            pltpu.VMEM((2, 3) + block, f32),
            pltpu.VMEM(block, f32),
            pltpu.VMEM(block, f32),
            pltpu.VMEM(block, f32),
            pltpu.VMEM(block, f32),
            pltpu.VMEM(block, f32),
            pltpu.VMEM((2,) + block, f32),
            pltpu.VMEM((6,) + block, f32),
            dma((19,)),
            dma((8, 2, 3)),
            dma((8, 2, 3)),
            dma((8, 2)),
            dma((8, 2)),
        ],
        compiler_params=pltpu.CompilerParams(
            collective_id=0, has_side_effects=True, vmem_limit_bytes=60 * 1024 * 1024
        ),
        name="window",
    )(
        forward_state, adjoint_state, lame_lambda, lame_mu, buoyancy,
        source_x, source_y, source_z, source_wavelet, absorb_width,
        receiver_x.reshape(1, -1), receiver_y.reshape(1, -1), receiver_residual,
    )
    return pl.pallas_call(
        hand_on,
        out_shape=shapes,
        in_specs=[hbm] * 3,
        out_specs=[hbm] * 3,
        scratch_shapes=[dma((3,))],
        compiler_params=pltpu.CompilerParams(vmem_limit_bytes=60 * 1024 * 1024),
        name="hand_on",
    )(*grads)


def solution(mesh):
    volume = P("gx", "gy", None)
    state = P(None, "gx", "gy", None)
    return jax.shard_map(
        local,
        mesh=mesh,
        in_specs=(state, state, volume, volume, volume) + (P(),) * 8,
        out_specs=(volume, volume, volume),
        check_vma=False,
    )
```

```python
import jax
import jax.numpy as jnp
from jax import lax
from jax.experimental import pallas as pl
from jax.experimental.pallas import tpu as pltpu
from jax.sharding import PartitionSpec as P

REC_DEPTH = 6
COEFS = (1225.0 / 1024.0, -245.0 / 3072.0, 49.0 / 5120.0, -5.0 / 7168.0)
TIME_STEP = 0.2
DAMPING = 0.3
MESH = pl.DeviceIdType.MESH

FS0, FV1, FS1, FV2, AS0, AV1, AS1, AV0 = range(8)
VELOCITY = (FV1, FV2, AV1, AV0)
UP, DOWN = 0, 1


def layers(e, way, c):
    backward = (c == 0) if e in VELOCITY else (c != 0)
    return 4 if backward == (way == UP) else 3


def diff(load, forward):
    total = None
    for order, coef in enumerate(COEFS, 1):
        high, low = (order, 1 - order) if forward else (order - 1, -order)
        term = coef * (load(high) - load(low))
        total = term if total is None else total + term
    return total


def kernel(
    fwd, adj, lam_in, mu_in, buo_in, src_x, src_y, src_z, src_w, width_in, rec_x, rec_y, residual,
    g_lam, g_mu, g_rho,
    px, py, ys, yr, szz, vel0, lam, mu, buo, damp, src, rinj, rates1,
    load_sem, xs_sem, xr_sem, ys_sem, yr_sem,
):
    gx, gy = lax.axis_index("gx"), lax.axis_index("gy")
    nx, ny = lax.axis_size("gx"), lax.axis_size("gy")
    cells_x, cells_y, depth = buo.shape
    pairs = cells_x // 2
    anchor_x, anchor_y = gx * cells_x, gy * cells_y
    total_x, total_y = nx * cells_x, ny * cells_y
    has = {("gx", UP): gx < nx - 1, ("gx", DOWN): gx > 0, ("gy", UP): gy < ny - 1, ("gy", DOWN): gy > 0}
    place = {"gx": gx, "gy": gy}

    def neighbour(axis, way):
        return {axis: place[axis] + (1 if way == UP else -1)}

    loads = {}

    def load(name, source, target):
        copy = pltpu.make_async_copy(source, target, load_sem.at[len(loads)])
        copy.start()
        loads[name] = copy

    middle, rows = pl.ds(4, cells_x), pl.ds(8, cells_y)
    for chain, (state, e) in enumerate(((fwd, FS0), (adj, AS0))):
        for c, k in enumerate((3, 6, 7)):
            load(("px", e, c), state.at[k], px.at[e, c, middle])
        for c, k in enumerate((4, 6, 8)):
            load(("py", e, c), state.at[k], py.at[e, c, :, rows])
    for chain, (state, e) in enumerate(((fwd, FS0), (adj, AS0))):
        load(("szz", e), state.at[5], szz.at[e])
        load(("vel", e), state.at[pl.ds(0, 3)], vel0.at[chain])
    load("buo", buo_in, buo)
    load("lam", lam_in, lam)
    load("mu", mu_in, mu)

    barrier = pltpu.get_barrier_semaphore()
    for (axis, way), there in has.items():
        @pl.when(there)
        def _(axis=axis, way=way):
            pl.semaphore_signal(barrier, inc=1, device_id=neighbour(axis, way), device_id_type=MESH)

    row = lax.broadcasted_iota(jnp.int32, (cells_y, depth), 0)
    lane = lax.broadcasted_iota(jnp.int32, (cells_y, depth), 1)
    coord_y = anchor_y + row

    def set_damping():
        width = width_in[0].astype(jnp.float32)

        def taper(dist):
            frac = jnp.maximum(width - dist.astype(jnp.float32), 0.0) / width
            return jnp.exp(-DAMPING * frac * frac)

        taper_y = taper(jnp.minimum(coord_y, total_y - 1 - coord_y))
        taper_z = taper(depth - 1 - lane)

        def plane(p, carry):
            coord_x = jnp.zeros((cells_y, depth), jnp.int32) + (anchor_x + p)
            damp[p] = taper(jnp.minimum(coord_x, total_x - 1 - coord_x)) * taper_y * taper_z
            return carry

        lax.fori_loop(0, cells_x, plane, 0)

    def set_injections():
        rec_row = anchor_y + lax.broadcasted_iota(jnp.int32, (cells_y, rec_x.shape[1]), 0) == rec_y[...]

        def plane(p, carry):
            total = jnp.zeros((cells_y, depth), jnp.float32)
            for s in range(src_x.shape[0]):
                amount = jnp.where(src_x[s] == anchor_x + p, TIME_STEP * src_w[s], 0.0)
                hit = (coord_y == src_y[s]) & (lane == src_z[s])
                total = total + jnp.where(hit, amount, 0.0)
            src[p] = total
            for t in range(2):
                amounts = jnp.where(rec_x[...] == anchor_x + p, TIME_STEP * residual[pl.ds(t, 1), :], 0.0)
                column = jnp.sum(jnp.where(rec_row, amounts, 0.0), axis=1, keepdims=True)
                rinj[t, p] = jnp.where(lane == REC_DEPTH, column, 0.0)
            return carry

        lax.fori_loop(0, cells_x, plane, 0)

    def set_zeros():
        for way in (UP, DOWN):
            @pl.when(jnp.logical_not(has["gx", 1 - way]))
            def _(way=way):
                def fill(e, carry):
                    px[e, :, pl.ds(0 if way == UP else 4 + cells_x, 4)] = jnp.zeros((3, 4, cells_y, depth), jnp.float32)
                    return carry
                lax.fori_loop(0, 8, fill, 0)

            @pl.when(jnp.logical_not(has["gy", 1 - way]))
            def _(way=way):
                def fill(e, carry):
                    yr[e, way] = jnp.zeros(yr.shape[2:], jnp.float32)
                    return carry
                lax.fori_loop(0, 8, fill, 0)

    def x_copy(e, way, c, peer):
        n = layers(e, way, c)
        if way == UP:
            source, target = pl.ds(4 + cells_x - n, n), pl.ds(4 - n, n)
        else:
            source, target = pl.ds(4, n), pl.ds(4 + cells_x, n)
        return pltpu.make_async_remote_copy(
            px.at[e, c, source], px.at[e, c, target], xs_sem.at[e, way, c], xr_sem.at[e, way, c],
            device_id=neighbour("gx", peer), device_id_type=MESH,
        )

    def y_copy(e, way, peer):
        return pltpu.make_async_remote_copy(
            ys.at[e, way], yr.at[e, way], ys_sem.at[e, way], yr_sem.at[e, way],
            device_id=neighbour("gy", peer), device_id_type=MESH,
        )

    odd_block = lax.rem(gx, 2)
    is_near = {UP: odd_block == 0, DOWN: odd_block == 1}

    def x_side(near, way):
        there = is_near[way] if near else jnp.logical_not(is_near[way])
        return jnp.logical_and(there, has["gx", way])

    def send_x(e, near):
        for way in (UP, DOWN):
            @pl.when(x_side(near, way))
            def _(way=way):
                for c in range(3):
                    x_copy(e, way, c, way).start()

    def sent_x(e, near):
        for way in (UP, DOWN):
            @pl.when(x_side(near, way))
            def _(way=way):
                for c in range(3):
                    x_copy(e, way, c, way).wait_send()

    def receive_x(e, near):
        for way in (UP, DOWN):
            @pl.when(x_side(near, 1 - way))
            def _(way=way):
                for c in range(3):
                    x_copy(e, way, c, 1 - way).wait_recv()

    def send_y(e):
        for way in (UP, DOWN):
            @pl.when(has["gy", way])
            def _(way=way):
                y_copy(e, way, way).start()

    def sent_y(e):
        for way in (UP, DOWN):
            @pl.when(has["gy", way])
            def _(way=way):
                y_copy(e, way, way).wait_send()

    def receive_y(e):
        for way in (UP, DOWN):
            @pl.when(has["gy", 1 - way])
            def _(way=way):
                y_copy(e, way, 1 - way).wait_recv()

        def unpack(q, odd, p):
            for c in range(3):
                tile, part = slot(c, q, odd)
                py[e, c, p, pl.ds(4, 4), :] = yr[e, UP, tile, part, :]
                py[e, c, p, pl.ds(8 + cells_y, 4), :] = yr[e, DOWN, tile, part, :]
        by_plane(unpack)

    def slot(c, q, odd):
        if c < 2:
            return 2 * q + odd, pl.ds(4 * c, 4)
        return cells_x + q, pl.ds(4 * odd, 4)

    def pack(e, c, q, odd, value):
        tile, part = slot(c, q, odd)
        ys[e, UP, tile, part, :] = value[cells_y - 4:]
        ys[e, DOWN, tile, part, :] = value[:4]

    def store_y(e, c, q, odd, value):
        py[e, c, 2 * q + odd, rows, :] = value
        pack(e, c, q, odd, value)

    def by_plane(body):
        def step(q, carry):
            for odd in range(2):
                body(q, odd, 2 * q + odd)
            return carry
        lax.fori_loop(0, pairs, step, 0)

    half = pairs // 2

    def stage(e, body, target=None):
        receive_y(e)
        receive_x(e, True)

        def step(i, carry):
            @pl.when(i == half)
            def _():
                if target is not None:
                    send_x(target, True)
                receive_x(e, False)

            q = lax.rem(i + half * (1 - odd_block), pairs)
            for odd in range(2):
                body(q, odd, 2 * q + odd)
            return carry

        lax.fori_loop(0, pairs, step, 0)
        if target is not None:
            send_x(target, False)
            send_y(target)

    def diff_x(e, c, p, forward):
        return diff(lambda k: px[e, c, p + (4 + k)], forward)

    def diff_y(e, c, p, forward):
        return diff(lambda k: py[e, c, p, pl.ds(8 + k, cells_y), :], forward)

    def diff_z(value, forward):
        def at(k):
            if k == 0:
                return value
            moved = pltpu.roll(value, (-k) % depth, 1)
            return jnp.where(lane < depth - k if k > 0 else lane >= -k, moved, 0.0)
        return diff(at, forward)

    def center_x(e, c, p):
        return px[e, c, p + 4]

    def center_y(e, c, p):
        return py[e, c, p, rows, :]

    def stresses(e, p):
        return (
            center_x(e, 0, p), center_y(e, 0, p), szz[e, p],
            center_x(e, 1, p), center_x(e, 2, p), center_y(e, 2, p),
        )

    def velocity_half(e, target, before):
        def body(q, odd, p):
            s = stresses(e, p)
            force = (
                diff_x(e, 0, p, True) + diff_y(e, 1, p, False) + diff_z(s[4], False),
                diff_x(e, 1, p, False) + diff_y(e, 0, p, True) + diff_z(s[5], False),
                diff_x(e, 2, p, False) + diff_y(e, 2, p, False) + diff_z(s[2], True),
            )
            scaled = TIME_STEP * buo[p]
            for c in range(3):
                value = damp[p] * (before(c, p) + scaled * force[c])
                px[target, c, p + 4] = value
                store_y(target, c, q, odd, value)
        return body

    def strain(e, p):
        vx, vy, vz = (center_x(e, c, p) for c in range(3))
        return (
            diff_x(e, 0, p, False),
            diff_y(e, 1, p, False),
            diff_z(vz, False),
            diff_y(e, 0, p, True) + diff_x(e, 1, p, True),
            diff_z(vx, True) + diff_x(e, 2, p, True),
            diff_z(vy, True) + diff_y(e, 2, p, True),
        )

    def stress_half(e, rates, p):
        s = stresses(e, p)
        normal = lam[p] * (rates[0] + rates[1] + rates[2])
        shear = TIME_STEP * mu[p]
        return [
            damp[p] * (s[k] + (TIME_STEP * normal + 2.0 * shear * rates[k])) for k in range(3)
        ] + [damp[p] * (s[k] + shear * rates[k]) for k in range(3, 6)]

    def store_stress(e, q, odd, p, s):
        for c, k in enumerate((0, 3, 4)):
            px[e, c, p + 4] = s[k]
        for c, k in enumerate((1, 3, 5)):
            store_y(e, c, q, odd, s[k])
        szz[e, p] = s[2]

    def forward_stress(q, odd, p):
        rates = strain(FV1, p)
        for k in range(6):
            rates1[k, p] = rates[k]
        s = stress_half(FS0, rates, p)
        for k in range(3):
            s[k] = s[k] + src[p]
        store_stress(FS1, q, odd, p, s)

    def adjoint_stress(q, odd, p):
        store_stress(AS1, q, odd, p, stress_half(AS0, strain(AV1, p), p))

    def adjoint_velocity(e, t, c, p):
        value = center_x(e, c, p)
        return value + rinj[t, p] if c == 2 else value

    def density(q, odd, p):
        total = None
        for c in range(3):
            one = center_x(FV1, c, p)
            term = (
                adjoint_velocity(AV1, 0, c, p) * (center_x(FV2, c, p) - one)
                + adjoint_velocity(AV0, 1, c, p) * (one - vel0[0, c, p])
            )
            total = term if total is None else total + term
        g_rho[p] = total / TIME_STEP

    def image(rates, s):
        lam_term = (rates[0] + rates[1] + rates[2]) * (s[0] + s[1] + s[2])
        normal = rates[0] * s[0] + rates[1] * s[1] + rates[2] * s[2]
        return lam_term, 2.0 * normal + rates[3] * s[3] + rates[4] * s[4] + rates[5] * s[5]

    def image_one(q, odd, p):
        g_lam[p], g_mu[p] = image(strain(FV2, p), stresses(AS1, p))

    def image_two(q, odd, p):
        s = stress_half(AS1, strain(AV0, p), p)
        lam_term, mu_term = image([rates1[k, p] for k in range(6)], s)
        g_lam[p] = g_lam[p] + lam_term
        g_mu[p] = g_mu[p] + mu_term

    forward_one = velocity_half(FS0, FV1, lambda c, p: vel0[0, c, p])
    adjoint_one = velocity_half(AS0, AV1, lambda c, p: vel0[1, c, p])
    forward_two = velocity_half(FS1, FV2, lambda c, p: center_x(FV1, c, p))
    adjoint_two = velocity_half(AS1, AV0, lambda c, p: adjoint_velocity(AV1, 0, c, p))

    def ready(e):
        for c in range(3):
            loads["py", e, c].wait()

        def first(q, odd, p):
            for c in range(3):
                pack(e, c, q, odd, center_y(e, c, p))
        by_plane(first)
        for c in range(3):
            loads["px", e, c].wait()

    ready(FS0)
    ready(AS0)
    set_damping()
    pl.semaphore_wait(barrier, sum(there.astype(jnp.int32) for there in has.values()))
    def send_first(e):
        for near in (False, True):
            send_x(e, near)
        send_y(e)

    send_first(FS0)
    set_zeros()
    set_injections()
    for name, copy in loads.items():
        if name[0] not in ("px", "py"):
            copy.wait()
    sent_x(FS0, False)
    send_first(AS0)

    stage(FS0, forward_one, FV1)
    stage(AS0, adjoint_one, AV1)
    stage(FV1, forward_stress, FS1)
    stage(AV1, adjoint_stress, AS1)
    stage(FS1, forward_two, FV2)
    stage(AS1, adjoint_two, AV0)
    by_plane(density)
    stage(FV2, image_one)
    stage(AV0, image_two)

    for e in range(8):
        if e != FS0:
            sent_x(e, False)
        sent_x(e, True)
        sent_y(e)


def local(
    forward_state, adjoint_state, lame_lambda, lame_mu, buoyancy,
    source_x, source_y, source_z, source_wavelet,
    receiver_x, receiver_y, receiver_residual, absorb_width,
):
    block = buoyancy.shape
    cells_x, cells_y, depth = block
    f32 = jnp.float32
    hbm, vmem, smem = (pl.BlockSpec(memory_space=m) for m in (pl.ANY, pltpu.VMEM, pltpu.SMEM))
    dma = pltpu.SemaphoreType.DMA
    packed = (8, 2, cells_x + cells_x // 2, 8, depth)
    return pl.pallas_call(
        kernel,
        out_shape=[jax.ShapeDtypeStruct(block, f32)] * 3,
        in_specs=[hbm] * 5 + [smem] * 5 + [vmem] * 3,
        out_specs=[vmem] * 3,
        scratch_shapes=[
            pltpu.VMEM((8, 3, cells_x + 8, cells_y, depth), f32),
            pltpu.VMEM((8, 3, cells_x, cells_y + 16, depth), f32),
            pltpu.VMEM(packed, f32),
            pltpu.VMEM(packed, f32),
            pltpu.VMEM((8,) + block, f32),
            pltpu.VMEM((2, 3) + block, f32),
            pltpu.VMEM(block, f32),
            pltpu.VMEM(block, f32),
            pltpu.VMEM(block, f32),
            pltpu.VMEM(block, f32),
            pltpu.VMEM(block, f32),
            pltpu.VMEM((2,) + block, f32),
            pltpu.VMEM((6,) + block, f32),
            dma((19,)),
            dma((8, 2, 3)),
            dma((8, 2, 3)),
            dma((8, 2)),
            dma((8, 2)),
        ],
        compiler_params=pltpu.CompilerParams(
            collective_id=0, has_side_effects=True, vmem_limit_bytes=60 * 1024 * 1024
        ),
        name="window",
    )(
        forward_state, adjoint_state, lame_lambda, lame_mu, buoyancy,
        source_x, source_y, source_z, source_wavelet, absorb_width,
        receiver_x.reshape(1, -1), receiver_y.reshape(1, -1), receiver_residual,
    )


def solution(mesh):
    volume = P("gx", "gy", None)
    state = P(None, "gx", "gy", None)
    return jax.shard_map(
        local,
        mesh=mesh,
        in_specs=(state, state, volume, volume, volume) + (P(),) * 8,
        out_specs=(volume, volume, volume),
        check_vma=False,
    )
```

```python
import jax
import jax.numpy as jnp
from jax import lax
from jax.experimental import pallas as pl
from jax.experimental.pallas import tpu as pltpu
from jax.sharding import PartitionSpec as P

REC_DEPTH = 6
COEFS = (1225.0 / 1024.0, -245.0 / 3072.0, 49.0 / 5120.0, -5.0 / 7168.0)
TIME_STEP = 0.2
DAMPING = 0.3
MESH = pl.DeviceIdType.MESH

FS0, FV1, FS1, FV2, AS0, AV1, AS1, AV0 = range(8)
VELOCITY = (FV1, FV2, AV1, AV0)
UP, DOWN = 0, 1

RUN = 4
TO_RELAY = {(UP, 0): RUN, (UP, 1): 1 - RUN, (DOWN, 0): RUN - 1, (DOWN, 1): -RUN}
FROM_RELAY = {(UP, 0): 1 - RUN, (UP, 1): RUN, (DOWN, 0): -RUN, (DOWN, 1): RUN - 1}


def layers(e, way, c):
    backward = (c == 0) if e in VELOCITY else (c != 0)
    return 4 if backward == (way == UP) else 3


def diff(load, forward):
    total = None
    for order, coef in enumerate(COEFS, 1):
        high, low = (order, 1 - order) if forward else (order - 1, -order)
        term = coef * (load(high) - load(low))
        total = term if total is None else total + term
    return total


def kernel(
    fwd, adj, lam_in, mu_in, buo_in, src_x, src_y, src_z, src_w, width_in, rec_x, rec_y, residual,
    g_lam, g_mu, g_rho,
    px, py, ys, yr, relayed, szz, vel0, lam, mu, buo, damp, src, rinj, rates1,
    load_sem, xs_sem, xr_sem, ys_sem, yr_sem, hop_sem, forward_sem,
):
    gx, gy = lax.axis_index("gx"), lax.axis_index("gy")
    nx, ny = lax.axis_size("gx"), lax.axis_size("gy")
    cells_x, cells_y, depth = buo.shape
    pairs = cells_x // 2
    anchor_x, anchor_y = gx * cells_x, gy * cells_y
    total_x, total_y = nx * cells_x, ny * cells_y
    has = {("gx", UP): gx < nx - 1, ("gx", DOWN): gx > 0, ("gy", UP): gy < ny - 1, ("gy", DOWN): gy > 0}
    place = {"gx": gx, "gy": gy}

    def neighbour(axis, way):
        return {axis: place[axis] + (1 if way == UP else -1)}

    column, wraps = lax.rem(gy, RUN), ny > RUN
    at_end = {UP: column == RUN - 1, DOWN: column == 0}

    def direct(way):
        return jnp.logical_and(has["gy", way], jnp.logical_not(at_end[way])) if wraps else has["gy", way]

    def wrapped(way):
        return jnp.logical_and(has["gy", way], at_end[way])

    relays = (
        jnp.logical_and(column == RUN - 1, gy >= RUN),
        jnp.logical_and(column == 0, gy + RUN < ny),
    )
    peers = [(has["gx", way], neighbour("gx", way)) for way in (UP, DOWN)]
    peers += [(direct(way), neighbour("gy", way)) for way in (UP, DOWN)]
    if wraps:
        ends = jnp.logical_or(at_end[UP], at_end[DOWN])
        peers += [
            (jnp.logical_and(ends, gy + RUN < ny), {"gy": gy + RUN}),
            (jnp.logical_and(ends, gy >= RUN), {"gy": gy - RUN}),
            (at_end[DOWN], {"gy": gy + (RUN - 1)}),
            (at_end[UP], {"gy": gy - (RUN - 1)}),
        ]

    loads = {}

    def load(name, source, target):
        copy = pltpu.make_async_copy(source, target, load_sem.at[len(loads)])
        copy.start()
        loads[name] = copy

    middle, rows = pl.ds(4, cells_x), pl.ds(8, cells_y)
    for chain, (state, e) in enumerate(((fwd, FS0), (adj, AS0))):
        for c, k in enumerate((3, 6, 7)):
            load(("px", e, c), state.at[k], px.at[e, c, middle])
        for c, k in enumerate((4, 6, 8)):
            load(("py", e, c), state.at[k], py.at[e, c, :, rows])
    for chain, (state, e) in enumerate(((fwd, FS0), (adj, AS0))):
        load(("szz", e), state.at[5], szz.at[e])
        load(("vel", e), state.at[pl.ds(0, 3)], vel0.at[chain])
    load("buo", buo_in, buo)
    load("lam", lam_in, lam)
    load("mu", mu_in, mu)

    barrier = pltpu.get_barrier_semaphore()
    for there, device in peers:
        @pl.when(there)
        def _(device=device):
            pl.semaphore_signal(barrier, inc=1, device_id=device, device_id_type=MESH)

    row = lax.broadcasted_iota(jnp.int32, (cells_y, depth), 0)
    lane = lax.broadcasted_iota(jnp.int32, (cells_y, depth), 1)
    coord_y = anchor_y + row

    def set_damping():
        width = width_in[0].astype(jnp.float32)

        def taper(dist):
            frac = jnp.maximum(width - dist.astype(jnp.float32), 0.0) / width
            return jnp.exp(-DAMPING * frac * frac)

        taper_y = taper(jnp.minimum(coord_y, total_y - 1 - coord_y))
        taper_z = taper(depth - 1 - lane)

        def plane(p, carry):
            coord_x = jnp.zeros((cells_y, depth), jnp.int32) + (anchor_x + p)
            damp[p] = taper(jnp.minimum(coord_x, total_x - 1 - coord_x)) * taper_y * taper_z
            return carry

        lax.fori_loop(0, cells_x, plane, 0)

    def set_injections():
        rec_row = anchor_y + lax.broadcasted_iota(jnp.int32, (cells_y, rec_x.shape[1]), 0) == rec_y[...]

        def plane(p, carry):
            total = jnp.zeros((cells_y, depth), jnp.float32)
            for s in range(src_x.shape[0]):
                amount = jnp.where(src_x[s] == anchor_x + p, TIME_STEP * src_w[s], 0.0)
                hit = (coord_y == src_y[s]) & (lane == src_z[s])
                total = total + jnp.where(hit, amount, 0.0)
            src[p] = total
            for t in range(2):
                amounts = jnp.where(rec_x[...] == anchor_x + p, TIME_STEP * residual[pl.ds(t, 1), :], 0.0)
                column = jnp.sum(jnp.where(rec_row, amounts, 0.0), axis=1, keepdims=True)
                rinj[t, p] = jnp.where(lane == REC_DEPTH, column, 0.0)
            return carry

        lax.fori_loop(0, cells_x, plane, 0)

    def set_zeros():
        for way in (UP, DOWN):
            @pl.when(jnp.logical_not(has["gx", 1 - way]))
            def _(way=way):
                def fill(e, carry):
                    px[e, :, pl.ds(0 if way == UP else 4 + cells_x, 4)] = jnp.zeros((3, 4, cells_y, depth), jnp.float32)
                    return carry
                lax.fori_loop(0, 8, fill, 0)

            @pl.when(jnp.logical_not(has["gy", 1 - way]))
            def _(way=way):
                def fill(e, carry):
                    yr[e, way] = jnp.zeros(yr.shape[2:], jnp.float32)
                    return carry
                lax.fori_loop(0, 8, fill, 0)

    def x_copy(e, way, c, peer):
        n = layers(e, way, c)
        if way == UP:
            source, target = pl.ds(4 + cells_x - n, n), pl.ds(4 - n, n)
        else:
            source, target = pl.ds(4, n), pl.ds(4 + cells_x, n)
        return pltpu.make_async_remote_copy(
            px.at[e, c, source], px.at[e, c, target], xs_sem.at[e, way, c], xr_sem.at[e, way, c],
            device_id=neighbour("gx", peer), device_id_type=MESH,
        )

    def y_copy(e, way, peer):
        return pltpu.make_async_remote_copy(
            ys.at[e, way], yr.at[e, way], ys_sem.at[e, way, 0], yr_sem.at[e, way, 0],
            device_id=neighbour("gy", peer), device_id_type=MESH,
        )

    tiles = ys.shape[2] // 2

    def y_hop(e, way, part, step):
        return pltpu.make_async_remote_copy(
            ys.at[e, way, pl.ds(part * tiles, tiles)], relayed.at[e, way],
            ys_sem.at[e, way, part], hop_sem.at[e, way],
            device_id={"gy": gy + step}, device_id_type=MESH,
        )

    def y_forward(e, way, part, step):
        return pltpu.make_async_remote_copy(
            relayed.at[e, way], yr.at[e, way, pl.ds(part * tiles, tiles)],
            forward_sem.at[e, way], yr_sem.at[e, way, part],
            device_id={"gy": gy + step}, device_id_type=MESH,
        )

    def relay(e):
        for part, here in enumerate(relays):
            if wraps:
                @pl.when(here)
                def _(part=part):
                    for way in (UP, DOWN):
                        y_hop(e, way, part, -TO_RELAY[way, part]).wait_recv()
                        y_forward(e, way, part, FROM_RELAY[way, part]).start()

    odd_block = lax.rem(gx, 2)
    is_near = {UP: odd_block == 0, DOWN: odd_block == 1}

    def x_side(near, way):
        there = is_near[way] if near else jnp.logical_not(is_near[way])
        return jnp.logical_and(there, has["gx", way])

    def send_x(e, near):
        for way in (UP, DOWN):
            @pl.when(x_side(near, way))
            def _(way=way):
                for c in range(3):
                    x_copy(e, way, c, way).start()

    def sent_x(e, near):
        for way in (UP, DOWN):
            @pl.when(x_side(near, way))
            def _(way=way):
                for c in range(3):
                    x_copy(e, way, c, way).wait_send()

    def receive_x(e, near):
        for way in (UP, DOWN):
            @pl.when(x_side(near, 1 - way))
            def _(way=way):
                for c in range(3):
                    x_copy(e, way, c, 1 - way).wait_recv()

    def send_y(e):
        for way in (UP, DOWN):
            @pl.when(direct(way))
            def _(way=way):
                y_copy(e, way, way).start()

            if wraps:
                @pl.when(wrapped(way))
                def _(way=way):
                    for part in range(2):
                        y_hop(e, way, part, TO_RELAY[way, part]).start()

    def sent_y(e):
        for way in (UP, DOWN):
            @pl.when(direct(way))
            def _(way=way):
                y_copy(e, way, way).wait_send()

            if wraps:
                @pl.when(wrapped(way))
                def _(way=way):
                    for part in range(2):
                        y_hop(e, way, part, TO_RELAY[way, part]).wait_send()

        for part, here in enumerate(relays):
            if wraps:
                @pl.when(here)
                def _(part=part):
                    for way in (UP, DOWN):
                        y_forward(e, way, part, FROM_RELAY[way, part]).wait_send()

    def receive_y(e):
        for way in (UP, DOWN):
            @pl.when(direct(1 - way))
            def _(way=way):
                y_copy(e, way, 1 - way).wait_recv()

            if wraps:
                @pl.when(wrapped(1 - way))
                def _(way=way):
                    for part in range(2):
                        y_forward(e, way, part, -FROM_RELAY[way, part]).wait_recv()

        def unpack(q, odd, p):
            for c in range(3):
                tile, part = slot(c, q, odd)
                py[e, c, p, pl.ds(4, 4), :] = yr[e, UP, tile, part, :]
                py[e, c, p, pl.ds(8 + cells_y, 4), :] = yr[e, DOWN, tile, part, :]
        by_plane(unpack)

    def slot(c, q, odd):
        if c < 2:
            return 2 * q + odd, pl.ds(4 * c, 4)
        return cells_x + q, pl.ds(4 * odd, 4)

    def pack(e, c, q, odd, value):
        tile, part = slot(c, q, odd)
        ys[e, UP, tile, part, :] = value[cells_y - 4:]
        ys[e, DOWN, tile, part, :] = value[:4]

    def store_y(e, c, q, odd, value):
        py[e, c, 2 * q + odd, rows, :] = value
        pack(e, c, q, odd, value)

    def by_plane(body):
        def step(q, carry):
            for odd in range(2):
                body(q, odd, 2 * q + odd)
            return carry
        lax.fori_loop(0, pairs, step, 0)

    half = pairs // 2

    def stage(e, body, target=None, passing=None):
        receive_y(e)
        receive_x(e, True)

        def step(i, carry):
            @pl.when(i == half)
            def _():
                if target is not None:
                    send_x(target, True)
                if passing is not None:
                    relay(passing)
                receive_x(e, False)

            q = lax.rem(i + half * (1 - odd_block), pairs)
            for odd in range(2):
                body(q, odd, 2 * q + odd)
            return carry

        lax.fori_loop(0, pairs, step, 0)
        if target is not None:
            send_x(target, False)
            send_y(target)

    def diff_x(e, c, p, forward):
        return diff(lambda k: px[e, c, p + (4 + k)], forward)

    def diff_y(e, c, p, forward):
        return diff(lambda k: py[e, c, p, pl.ds(8 + k, cells_y), :], forward)

    def diff_z(value, forward):
        def at(k):
            if k == 0:
                return value
            moved = pltpu.roll(value, (-k) % depth, 1)
            return jnp.where(lane < depth - k if k > 0 else lane >= -k, moved, 0.0)
        return diff(at, forward)

    def center_x(e, c, p):
        return px[e, c, p + 4]

    def center_y(e, c, p):
        return py[e, c, p, rows, :]

    def stresses(e, p):
        return (
            center_x(e, 0, p), center_y(e, 0, p), szz[e, p],
            center_x(e, 1, p), center_x(e, 2, p), center_y(e, 2, p),
        )

    def velocity_half(e, target, before):
        def body(q, odd, p):
            s = stresses(e, p)
            force = (
                diff_x(e, 0, p, True) + diff_y(e, 1, p, False) + diff_z(s[4], False),
                diff_x(e, 1, p, False) + diff_y(e, 0, p, True) + diff_z(s[5], False),
                diff_x(e, 2, p, False) + diff_y(e, 2, p, False) + diff_z(s[2], True),
            )
            scaled = TIME_STEP * buo[p]
            for c in range(3):
                value = damp[p] * (before(c, p) + scaled * force[c])
                px[target, c, p + 4] = value
                store_y(target, c, q, odd, value)
        return body

    def strain(e, p):
        vx, vy, vz = (center_x(e, c, p) for c in range(3))
        return (
            diff_x(e, 0, p, False),
            diff_y(e, 1, p, False),
            diff_z(vz, False),
            diff_y(e, 0, p, True) + diff_x(e, 1, p, True),
            diff_z(vx, True) + diff_x(e, 2, p, True),
            diff_z(vy, True) + diff_y(e, 2, p, True),
        )

    def stress_half(e, rates, p):
        s = stresses(e, p)
        normal = lam[p] * (rates[0] + rates[1] + rates[2])
        shear = TIME_STEP * mu[p]
        return [
            damp[p] * (s[k] + (TIME_STEP * normal + 2.0 * shear * rates[k])) for k in range(3)
        ] + [damp[p] * (s[k] + shear * rates[k]) for k in range(3, 6)]

    def store_stress(e, q, odd, p, s):
        for c, k in enumerate((0, 3, 4)):
            px[e, c, p + 4] = s[k]
        for c, k in enumerate((1, 3, 5)):
            store_y(e, c, q, odd, s[k])
        szz[e, p] = s[2]

    def forward_stress(q, odd, p):
        rates = strain(FV1, p)
        for k in range(6):
            rates1[k, p] = rates[k]
        s = stress_half(FS0, rates, p)
        for k in range(3):
            s[k] = s[k] + src[p]
        store_stress(FS1, q, odd, p, s)

    def adjoint_stress(q, odd, p):
        store_stress(AS1, q, odd, p, stress_half(AS0, strain(AV1, p), p))

    def adjoint_velocity(e, t, c, p):
        value = center_x(e, c, p)
        return value + rinj[t, p] if c == 2 else value

    def density(q, odd, p):
        total = None
        for c in range(3):
            one = center_x(FV1, c, p)
            term = (
                adjoint_velocity(AV1, 0, c, p) * (center_x(FV2, c, p) - one)
                + adjoint_velocity(AV0, 1, c, p) * (one - vel0[0, c, p])
            )
            total = term if total is None else total + term
        g_rho[p] = total / TIME_STEP

    def image(rates, s):
        lam_term = (rates[0] + rates[1] + rates[2]) * (s[0] + s[1] + s[2])
        normal = rates[0] * s[0] + rates[1] * s[1] + rates[2] * s[2]
        return lam_term, 2.0 * normal + rates[3] * s[3] + rates[4] * s[4] + rates[5] * s[5]

    def image_one(q, odd, p):
        g_lam[p], g_mu[p] = image(strain(FV2, p), stresses(AS1, p))

    def image_two(q, odd, p):
        s = stress_half(AS1, strain(AV0, p), p)
        lam_term, mu_term = image([rates1[k, p] for k in range(6)], s)
        g_lam[p] = g_lam[p] + lam_term
        g_mu[p] = g_mu[p] + mu_term

    forward_one = velocity_half(FS0, FV1, lambda c, p: vel0[0, c, p])
    adjoint_one = velocity_half(AS0, AV1, lambda c, p: vel0[1, c, p])
    forward_two = velocity_half(FS1, FV2, lambda c, p: center_x(FV1, c, p))
    adjoint_two = velocity_half(AS1, AV0, lambda c, p: adjoint_velocity(AV1, 0, c, p))

    def ready(e):
        for c in range(3):
            loads["py", e, c].wait()

        def first(q, odd, p):
            for c in range(3):
                pack(e, c, q, odd, center_y(e, c, p))
        by_plane(first)
        for c in range(3):
            loads["px", e, c].wait()

    ready(FS0)
    ready(AS0)
    set_damping()
    pl.semaphore_wait(barrier, sum(there.astype(jnp.int32) for there, _ in peers))
    def send_first(e):
        for near in (False, True):
            send_x(e, near)
        send_y(e)

    send_first(FS0)
    set_zeros()
    set_injections()
    for name, copy in loads.items():
        if name[0] not in ("px", "py"):
            copy.wait()
    relay(FS0)
    sent_x(FS0, False)
    send_first(AS0)

    stage(FS0, forward_one, FV1, AS0)
    stage(AS0, adjoint_one, AV1, FV1)
    stage(FV1, forward_stress, FS1, AV1)
    stage(AV1, adjoint_stress, AS1, FS1)
    stage(FS1, forward_two, FV2, AS1)
    stage(AS1, adjoint_two, AV0, FV2)
    by_plane(density)
    stage(FV2, image_one, None, AV0)
    stage(AV0, image_two)

    for e in range(8):
        if e != FS0:
            sent_x(e, False)
        sent_x(e, True)
        sent_y(e)


def local(
    forward_state, adjoint_state, lame_lambda, lame_mu, buoyancy,
    source_x, source_y, source_z, source_wavelet,
    receiver_x, receiver_y, receiver_residual, absorb_width,
):
    block = buoyancy.shape
    cells_x, cells_y, depth = block
    f32 = jnp.float32
    hbm, vmem, smem = (pl.BlockSpec(memory_space=m) for m in (pl.ANY, pltpu.VMEM, pltpu.SMEM))
    dma = pltpu.SemaphoreType.DMA
    packed = (8, 2, cells_x + cells_x // 2, 8, depth)
    return pl.pallas_call(
        kernel,
        out_shape=[jax.ShapeDtypeStruct(block, f32)] * 3,
        in_specs=[hbm] * 5 + [smem] * 5 + [vmem] * 3,
        out_specs=[vmem] * 3,
        scratch_shapes=[
            pltpu.VMEM((8, 3, cells_x + 8, cells_y, depth), f32),
            pltpu.VMEM((8, 3, cells_x, cells_y + 16, depth), f32),
            pltpu.VMEM(packed, f32),
            pltpu.VMEM(packed, f32),
            pltpu.VMEM((8, 2, packed[2] // 2, 8, depth), f32),
            pltpu.VMEM((8,) + block, f32),
            pltpu.VMEM((2, 3) + block, f32),
            pltpu.VMEM(block, f32),
            pltpu.VMEM(block, f32),
            pltpu.VMEM(block, f32),
            pltpu.VMEM(block, f32),
            pltpu.VMEM(block, f32),
            pltpu.VMEM((2,) + block, f32),
            pltpu.VMEM((6,) + block, f32),
            dma((19,)),
            dma((8, 2, 3)),
            dma((8, 2, 3)),
            dma((8, 2, 2)),
            dma((8, 2, 2)),
            dma((8, 2)),
            dma((8, 2)),
        ],
        compiler_params=pltpu.CompilerParams(
            collective_id=0, has_side_effects=True, vmem_limit_bytes=60 * 1024 * 1024
        ),
        name="window",
    )(
        forward_state, adjoint_state, lame_lambda, lame_mu, buoyancy,
        source_x, source_y, source_z, source_wavelet, absorb_width,
        receiver_x.reshape(1, -1), receiver_y.reshape(1, -1), receiver_residual,
    )


def solution(mesh):
    volume = P("gx", "gy", None)
    state = P(None, "gx", "gy", None)
    return jax.shard_map(
        local,
        mesh=mesh,
        in_specs=(state, state, volume, volume, volume) + (P(),) * 8,
        out_specs=(volume, volume, volume),
        check_vma=False,
    )
```

```python
import jax
import jax.numpy as jnp
from jax import lax
from jax.experimental import pallas as pl
from jax.experimental.pallas import tpu as pltpu
from jax.sharding import PartitionSpec as P

REC_DEPTH = 6
COEFS = (1225.0 / 1024.0, -245.0 / 3072.0, 49.0 / 5120.0, -5.0 / 7168.0)
TIME_STEP = 0.2
DAMPING = 0.3
MESH = pl.DeviceIdType.MESH

FS0, FV1, FS1, FV2, AS0, AV1, AS1, AV0 = range(8)
VELOCITY = (FV1, FV2, AV1, AV0)
UP, DOWN = 0, 1


def layers(e, way, c):
    backward = (c == 0) if e in VELOCITY else (c != 0)
    return 4 if backward == (way == UP) else 3


def diff(load, forward):
    total = None
    for order, coef in enumerate(COEFS, 1):
        high, low = (order, 1 - order) if forward else (order - 1, -order)
        term = coef * (load(high) - load(low))
        total = term if total is None else total + term
    return total


def kernel(
    fwd, adj, lam_in, mu_in, buo_in, src_x, src_y, src_z, src_w, width_in, rec_x, rec_y, residual,
    grads,
    px, py, ys, yr, szz, vel0, lam, mu, buo, damp, src, rinj, rates1,
    load_sem, xs_sem, xr_sem, ys_sem, yr_sem,
):
    g_lam, g_mu, g_rho = (grads.at[k] for k in range(3))
    gx, gy = lax.axis_index("gx"), lax.axis_index("gy")
    nx, ny = lax.axis_size("gx"), lax.axis_size("gy")
    cells_x, cells_y, depth = buo.shape
    pairs = cells_x // 2
    anchor_x, anchor_y = gx * cells_x, gy * cells_y
    total_x, total_y = nx * cells_x, ny * cells_y
    has = {("gx", UP): gx < nx - 1, ("gx", DOWN): gx > 0, ("gy", UP): gy < ny - 1, ("gy", DOWN): gy > 0}
    place = {"gx": gx, "gy": gy}

    def neighbour(axis, way):
        return {axis: place[axis] + (1 if way == UP else -1)}

    loads = {}

    def load(name, source, target):
        copy = pltpu.make_async_copy(source, target, load_sem.at[len(loads)])
        copy.start()
        loads[name] = copy

    middle, rows = pl.ds(4, cells_x), pl.ds(8, cells_y)
    for chain, (state, e) in enumerate(((fwd, FS0), (adj, AS0))):
        for c, k in enumerate((3, 6, 7)):
            load(("px", e, c), state.at[k], px.at[e, c, middle])
        for c, k in enumerate((4, 6, 8)):
            load(("py", e, c), state.at[k], py.at[e, c, :, rows])
    for chain, (state, e) in enumerate(((fwd, FS0), (adj, AS0))):
        load(("szz", e), state.at[5], szz.at[e])
        load(("vel", e), state.at[pl.ds(0, 3)], vel0.at[chain])
    load("buo", buo_in, buo)
    load("lam", lam_in, lam)
    load("mu", mu_in, mu)

    barrier = pltpu.get_barrier_semaphore()
    for (axis, way), there in has.items():
        @pl.when(there)
        def _(axis=axis, way=way):
            pl.semaphore_signal(barrier, inc=1, device_id=neighbour(axis, way), device_id_type=MESH)

    row = lax.broadcasted_iota(jnp.int32, (cells_y, depth), 0)
    lane = lax.broadcasted_iota(jnp.int32, (cells_y, depth), 1)
    coord_y = anchor_y + row

    def set_damping():
        width = width_in[0].astype(jnp.float32)

        def taper(dist):
            frac = jnp.maximum(width - dist.astype(jnp.float32), 0.0) / width
            return jnp.exp(-DAMPING * frac * frac)

        taper_y = taper(jnp.minimum(coord_y, total_y - 1 - coord_y))
        taper_z = taper(depth - 1 - lane)

        def plane(p, carry):
            coord_x = jnp.zeros((cells_y, depth), jnp.int32) + (anchor_x + p)
            damp[p] = taper(jnp.minimum(coord_x, total_x - 1 - coord_x)) * taper_y * taper_z
            return carry

        lax.fori_loop(0, cells_x, plane, 0)

    def set_injections():
        rec_row = anchor_y + lax.broadcasted_iota(jnp.int32, (cells_y, rec_x.shape[1]), 0) == rec_y[...]

        def plane(p, carry):
            total = jnp.zeros((cells_y, depth), jnp.float32)
            for s in range(src_x.shape[0]):
                amount = jnp.where(src_x[s] == anchor_x + p, TIME_STEP * src_w[s], 0.0)
                hit = (coord_y == src_y[s]) & (lane == src_z[s])
                total = total + jnp.where(hit, amount, 0.0)
            src[p] = total
            for t in range(2):
                amounts = jnp.where(rec_x[...] == anchor_x + p, TIME_STEP * residual[pl.ds(t, 1), :], 0.0)
                column = jnp.sum(jnp.where(rec_row, amounts, 0.0), axis=1, keepdims=True)
                rinj[t, p] = jnp.where(lane == REC_DEPTH, column, 0.0)
            return carry

        lax.fori_loop(0, cells_x, plane, 0)

    def set_zeros():
        for way in (UP, DOWN):
            @pl.when(jnp.logical_not(has["gx", 1 - way]))
            def _(way=way):
                def fill(e, carry):
                    px[e, :, pl.ds(0 if way == UP else 4 + cells_x, 4)] = jnp.zeros((3, 4, cells_y, depth), jnp.float32)
                    return carry
                lax.fori_loop(0, 8, fill, 0)

            @pl.when(jnp.logical_not(has["gy", 1 - way]))
            def _(way=way):
                def fill(e, carry):
                    yr[e, way] = jnp.zeros(yr.shape[2:], jnp.float32)
                    return carry
                lax.fori_loop(0, 8, fill, 0)

    def x_copy(e, way, c, peer):
        n = layers(e, way, c)
        if way == UP:
            source, target = pl.ds(4 + cells_x - n, n), pl.ds(4 - n, n)
        else:
            source, target = pl.ds(4, n), pl.ds(4 + cells_x, n)
        return pltpu.make_async_remote_copy(
            px.at[e, c, source], px.at[e, c, target], xs_sem.at[e, way, c], xr_sem.at[e, way, c],
            device_id=neighbour("gx", peer), device_id_type=MESH,
        )

    odd_block = lax.rem(gx, 2)
    is_near = {UP: odd_block == 0, DOWN: odd_block == 1}

    def x_side(near, way):
        there = is_near[way] if near else jnp.logical_not(is_near[way])
        return jnp.logical_and(there, has["gx", way])

    def send_x(e, near):
        for way in (UP, DOWN):
            @pl.when(x_side(near, way))
            def _(way=way):
                for c in range(3):
                    x_copy(e, way, c, way).start()

    def sent_x(e, near):
        for way in (UP, DOWN):
            @pl.when(x_side(near, way))
            def _(way=way):
                for c in range(3):
                    x_copy(e, way, c, way).wait_send()

    def receive_x(e, near):
        for way in (UP, DOWN):
            @pl.when(x_side(near, 1 - way))
            def _(way=way):
                for c in range(3):
                    x_copy(e, way, c, 1 - way).wait_recv()

    half = pairs // 2
    part_of = {True: 1 - odd_block, False: odd_block}
    tiles = ys.shape[2] // 2

    def y_copy(e, way, near, peer):
        part = pl.ds(part_of[near] * tiles, tiles)
        k = 0 if near else 1
        return pltpu.make_async_remote_copy(
            ys.at[e, way, part], yr.at[e, way, part], ys_sem.at[e, way, k], yr_sem.at[e, way, k],
            device_id=neighbour("gy", peer), device_id_type=MESH,
        )

    def send_y(e, near):
        for way in (UP, DOWN):
            @pl.when(has["gy", way])
            def _(way=way):
                y_copy(e, way, near, way).start()

    def sent_y(e, near):
        for way in (UP, DOWN):
            @pl.when(has["gy", way])
            def _(way=way):
                y_copy(e, way, near, way).wait_send()

    def receive_y(e, near):
        for way in (UP, DOWN):
            @pl.when(has["gy", 1 - way])
            def _(way=way):
                y_copy(e, way, near, 1 - way).wait_recv()

        def unpack(i, carry):
            q = part_of[near] * half + i
            for odd in range(2):
                p = 2 * q + odd
                for c in range(3):
                    tile, rows4 = slot(c, q, odd)
                    py[e, c, p, pl.ds(4, 4), :] = yr[e, UP, tile, rows4, :]
                    py[e, c, p, pl.ds(8 + cells_y, 4), :] = yr[e, DOWN, tile, rows4, :]
            return carry

        lax.fori_loop(0, half, unpack, 0)

    def slot(c, q, odd):
        start, inside = lax.div(q, half) * tiles, lax.rem(q, half)
        if c < 2:
            return start + 2 * inside + odd, pl.ds(4 * c, 4)
        return start + 2 * half + inside, pl.ds(4 * odd, 4)

    def pack(e, c, q, odd, value):
        tile, part = slot(c, q, odd)
        ys[e, UP, tile, part, :] = value[cells_y - 4:]
        ys[e, DOWN, tile, part, :] = value[:4]

    def store_y(e, c, q, odd, value):
        py[e, c, 2 * q + odd, rows, :] = value
        pack(e, c, q, odd, value)

    def by_plane(body):
        def step(q, carry):
            for odd in range(2):
                body(q, odd, 2 * q + odd)
            return carry
        lax.fori_loop(0, pairs, step, 0)

    def stage(e, body, target=None):
        receive_y(e, True)
        receive_x(e, True)

        def step(i, carry):
            @pl.when(i == half)
            def _():
                if target is not None:
                    send_y(target, True)
                    send_x(target, True)
                receive_y(e, False)
                receive_x(e, False)

            q = lax.rem(i + half * part_of[True], pairs)
            for odd in range(2):
                body(q, odd, 2 * q + odd)
            return carry

        lax.fori_loop(0, pairs, step, 0)
        if target is not None:
            send_x(target, False)
            send_y(target, False)

    def diff_x(e, c, p, forward):
        return diff(lambda k: px[e, c, p + (4 + k)], forward)

    def diff_y(e, c, p, forward):
        return diff(lambda k: py[e, c, p, pl.ds(8 + k, cells_y), :], forward)

    def diff_z(value, forward):
        def at(k):
            if k == 0:
                return value
            moved = pltpu.roll(value, (-k) % depth, 1)
            return jnp.where(lane < depth - k if k > 0 else lane >= -k, moved, 0.0)
        return diff(at, forward)

    def center_x(e, c, p):
        return px[e, c, p + 4]

    def center_y(e, c, p):
        return py[e, c, p, rows, :]

    def stresses(e, p):
        return (
            center_x(e, 0, p), center_y(e, 0, p), szz[e, p],
            center_x(e, 1, p), center_x(e, 2, p), center_y(e, 2, p),
        )

    def velocity_half(e, target, before):
        def body(q, odd, p):
            s = stresses(e, p)
            force = (
                diff_x(e, 0, p, True) + diff_y(e, 1, p, False) + diff_z(s[4], False),
                diff_x(e, 1, p, False) + diff_y(e, 0, p, True) + diff_z(s[5], False),
                diff_x(e, 2, p, False) + diff_y(e, 2, p, False) + diff_z(s[2], True),
            )
            scaled = TIME_STEP * buo[p]
            for c in range(3):
                value = damp[p] * (before(c, p) + scaled * force[c])
                px[target, c, p + 4] = value
                store_y(target, c, q, odd, value)
        return body

    def strain(e, p):
        vx, vy, vz = (center_x(e, c, p) for c in range(3))
        return (
            diff_x(e, 0, p, False),
            diff_y(e, 1, p, False),
            diff_z(vz, False),
            diff_y(e, 0, p, True) + diff_x(e, 1, p, True),
            diff_z(vx, True) + diff_x(e, 2, p, True),
            diff_z(vy, True) + diff_y(e, 2, p, True),
        )

    def stress_half(e, rates, p):
        s = stresses(e, p)
        normal = lam[p] * (rates[0] + rates[1] + rates[2])
        shear = TIME_STEP * mu[p]
        return [
            damp[p] * (s[k] + (TIME_STEP * normal + 2.0 * shear * rates[k])) for k in range(3)
        ] + [damp[p] * (s[k] + shear * rates[k]) for k in range(3, 6)]

    def store_stress(e, q, odd, p, s):
        for c, k in enumerate((0, 3, 4)):
            px[e, c, p + 4] = s[k]
        for c, k in enumerate((1, 3, 5)):
            store_y(e, c, q, odd, s[k])
        szz[e, p] = s[2]

    def forward_stress(q, odd, p):
        rates = strain(FV1, p)
        for k in range(6):
            rates1[k, p] = rates[k]
        s = stress_half(FS0, rates, p)
        for k in range(3):
            s[k] = s[k] + src[p]
        store_stress(FS1, q, odd, p, s)

    def adjoint_stress(q, odd, p):
        store_stress(AS1, q, odd, p, stress_half(AS0, strain(AV1, p), p))

    def adjoint_velocity(e, t, c, p):
        value = center_x(e, c, p)
        return value + rinj[t, p] if c == 2 else value

    def density(q, odd, p):
        total = None
        for c in range(3):
            one = center_x(FV1, c, p)
            term = (
                adjoint_velocity(AV1, 0, c, p) * (center_x(FV2, c, p) - one)
                + adjoint_velocity(AV0, 1, c, p) * (one - vel0[0, c, p])
            )
            total = term if total is None else total + term
        g_rho[p] = total / TIME_STEP

    def image(rates, s):
        lam_term = (rates[0] + rates[1] + rates[2]) * (s[0] + s[1] + s[2])
        normal = rates[0] * s[0] + rates[1] * s[1] + rates[2] * s[2]
        return lam_term, 2.0 * normal + rates[3] * s[3] + rates[4] * s[4] + rates[5] * s[5]

    def image_one(q, odd, p):
        g_lam[p], g_mu[p] = image(strain(FV2, p), stresses(AS1, p))

    def image_two(q, odd, p):
        s = stress_half(AS1, strain(AV0, p), p)
        lam_term, mu_term = image([rates1[k, p] for k in range(6)], s)
        g_lam[p] = g_lam[p] + lam_term
        g_mu[p] = g_mu[p] + mu_term

    forward_one = velocity_half(FS0, FV1, lambda c, p: vel0[0, c, p])
    adjoint_one = velocity_half(AS0, AV1, lambda c, p: vel0[1, c, p])
    forward_two = velocity_half(FS1, FV2, lambda c, p: center_x(FV1, c, p))
    adjoint_two = velocity_half(AS1, AV0, lambda c, p: adjoint_velocity(AV1, 0, c, p))

    def ready(e):
        for c in range(3):
            loads["py", e, c].wait()

        def first(q, odd, p):
            for c in range(3):
                pack(e, c, q, odd, center_y(e, c, p))
        by_plane(first)
        for c in range(3):
            loads["px", e, c].wait()

    ready(FS0)
    ready(AS0)
    set_damping()
    pl.semaphore_wait(barrier, sum(there.astype(jnp.int32) for there in has.values()))
    def send_first(e):
        send_x(e, False)
        send_y(e, True)
        send_x(e, True)
        send_y(e, False)

    send_first(FS0)
    set_zeros()
    set_injections()
    for name, copy in loads.items():
        if name[0] not in ("px", "py"):
            copy.wait()
    sent_x(FS0, False)
    send_first(AS0)

    stage(FS0, forward_one, FV1)
    stage(AS0, adjoint_one, AV1)
    stage(FV1, forward_stress, FS1)
    stage(AV1, adjoint_stress, AS1)
    stage(FS1, forward_two, FV2)
    stage(AS1, adjoint_two, AV0)
    by_plane(density)
    stage(FV2, image_one)
    stage(AV0, image_two)

    for e in range(8):
        if e != FS0:
            sent_x(e, False)
        sent_x(e, True)
        sent_y(e, True)
        sent_y(e, False)


def local(
    forward_state, adjoint_state, lame_lambda, lame_mu, buoyancy,
    source_x, source_y, source_z, source_wavelet,
    receiver_x, receiver_y, receiver_residual, absorb_width,
):
    block = buoyancy.shape
    cells_x, cells_y, depth = block
    f32 = jnp.float32
    hbm, vmem, smem = (pl.BlockSpec(memory_space=m) for m in (pl.ANY, pltpu.VMEM, pltpu.SMEM))
    dma = pltpu.SemaphoreType.DMA
    packed = (8, 2, cells_x + cells_x // 2, 8, depth)
    grads = pl.pallas_call(
        kernel,
        out_shape=jax.ShapeDtypeStruct((3,) + block, f32),
        in_specs=[hbm] * 5 + [smem] * 5 + [vmem] * 3,
        out_specs=vmem,
        scratch_shapes=[
            pltpu.VMEM((8, 3, cells_x + 8, cells_y, depth), f32),
            pltpu.VMEM((8, 3, cells_x, cells_y + 16, depth), f32),
            pltpu.VMEM(packed, f32),
            pltpu.VMEM(packed, f32),
            pltpu.VMEM((8,) + block, f32),
            pltpu.VMEM((2, 3) + block, f32),
            pltpu.VMEM(block, f32),
            pltpu.VMEM(block, f32),
            pltpu.VMEM(block, f32),
            pltpu.VMEM(block, f32),
            pltpu.VMEM(block, f32),
            pltpu.VMEM((2,) + block, f32),
            pltpu.VMEM((6,) + block, f32),
            dma((19,)),
            dma((8, 2, 3)),
            dma((8, 2, 3)),
            dma((8, 2, 2)),
            dma((8, 2, 2)),
        ],
        compiler_params=pltpu.CompilerParams(
            collective_id=0, has_side_effects=True, vmem_limit_bytes=60 * 1024 * 1024
        ),
        name="window",
    )(
        forward_state, adjoint_state, lame_lambda, lame_mu, buoyancy,
        source_x, source_y, source_z, source_wavelet, absorb_width,
        receiver_x.reshape(1, -1), receiver_y.reshape(1, -1), receiver_residual,
    )
    return grads[0], grads[1], grads[2]


def solution(mesh):
    volume = P("gx", "gy", None)
    state = P(None, "gx", "gy", None)
    return jax.shard_map(
        local,
        mesh=mesh,
        in_specs=(state, state, volume, volume, volume) + (P(),) * 8,
        out_specs=(volume, volume, volume),
        check_vma=False,
    )
```

```python
import jax
import jax.numpy as jnp
from jax import lax
from jax.experimental import pallas as pl
from jax.experimental.pallas import tpu as pltpu
from jax.sharding import PartitionSpec as P

REC_DEPTH = 6
COEFS = (1225.0 / 1024.0, -245.0 / 3072.0, 49.0 / 5120.0, -5.0 / 7168.0)
TIME_STEP = 0.2
DAMPING = 0.3
MESH = pl.DeviceIdType.MESH

FS0, FV1, FS1, FV2, AS0, AV1, AS1, AV0 = range(8)
VELOCITY = (FV1, FV2, AV1, AV0)
UP, DOWN = 0, 1


def layers(e, way, c):
    backward = (c == 0) if e in VELOCITY else (c != 0)
    return 4 if backward == (way == UP) else 3


def diff(load, forward):
    total = None
    for order, coef in enumerate(COEFS, 1):
        high, low = (order, 1 - order) if forward else (order - 1, -order)
        term = coef * (load(high) - load(low))
        total = term if total is None else total + term
    return total


def kernel(
    fwd, adj, lam_in, mu_in, buo_in, src_x, src_y, src_z, src_w, width_in, rec_x, rec_y, residual,
    grads,
    px, py, ys, yr, szz, vel0, lam, mu, buo, damp, src, rinj, rates1,
    load_sem, xs_sem, xr_sem, ys_sem, yr_sem,
):
    g_lam, g_mu, g_rho = (grads.at[k] for k in range(3))
    gx, gy = lax.axis_index("gx"), lax.axis_index("gy")
    nx, ny = lax.axis_size("gx"), lax.axis_size("gy")
    cells_x, cells_y, depth = buo.shape
    pairs = cells_x // 2
    anchor_x, anchor_y = gx * cells_x, gy * cells_y
    total_x, total_y = nx * cells_x, ny * cells_y
    has = {("gx", UP): gx < nx - 1, ("gx", DOWN): gx > 0, ("gy", UP): gy < ny - 1, ("gy", DOWN): gy > 0}
    place = {"gx": gx, "gy": gy}

    def neighbour(axis, way):
        return {axis: place[axis] + (1 if way == UP else -1)}

    barrier = pltpu.get_barrier_semaphore()
    for (axis, way), there in has.items():
        @pl.when(there)
        def _(axis=axis, way=way):
            pl.semaphore_signal(barrier, inc=1, device_id=neighbour(axis, way), device_id_type=MESH)

    loads = {}

    def load(name, source, target):
        copy = pltpu.make_async_copy(source, target, load_sem.at[len(loads)])
        copy.start()
        loads[name] = copy

    middle, rows = pl.ds(4, cells_x), pl.ds(8, cells_y)
    for chain, (state, e) in enumerate(((fwd, FS0), (adj, AS0))):
        for c, k in enumerate((3, 6, 7)):
            load(("px", e, c), state.at[k], px.at[e, c, middle])
        for c, k in enumerate((4, 6, 8)):
            load(("py", e, c), state.at[k], py.at[e, c, :, rows])
    for chain, (state, e) in enumerate(((fwd, FS0), (adj, AS0))):
        load(("szz", e), state.at[5], szz.at[e])
        load(("vel", e), state.at[pl.ds(0, 3)], vel0.at[chain])
    load("buo", buo_in, buo)
    load("lam", lam_in, lam)
    load("mu", mu_in, mu)

    row = lax.broadcasted_iota(jnp.int32, (cells_y, depth), 0)
    lane = lax.broadcasted_iota(jnp.int32, (cells_y, depth), 1)
    coord_y = anchor_y + row

    def set_damping():
        width = width_in[0].astype(jnp.float32)

        def taper(dist):
            frac = jnp.maximum(width - dist.astype(jnp.float32), 0.0) / width
            return jnp.exp(-DAMPING * frac * frac)

        taper_y = taper(jnp.minimum(coord_y, total_y - 1 - coord_y))
        taper_z = taper(depth - 1 - lane)

        def plane(p, carry):
            coord_x = jnp.zeros((cells_y, depth), jnp.int32) + (anchor_x + p)
            damp[p] = taper(jnp.minimum(coord_x, total_x - 1 - coord_x)) * taper_y * taper_z
            return carry

        lax.fori_loop(0, cells_x, plane, 0)

    def set_injections():
        rec_row = anchor_y + lax.broadcasted_iota(jnp.int32, (cells_y, rec_x.shape[1]), 0) == rec_y[...]

        def plane(p, carry):
            total = jnp.zeros((cells_y, depth), jnp.float32)
            for s in range(src_x.shape[0]):
                amount = jnp.where(src_x[s] == anchor_x + p, TIME_STEP * src_w[s], 0.0)
                hit = (coord_y == src_y[s]) & (lane == src_z[s])
                total = total + jnp.where(hit, amount, 0.0)
            src[p] = total
            for t in range(2):
                amounts = jnp.where(rec_x[...] == anchor_x + p, TIME_STEP * residual[pl.ds(t, 1), :], 0.0)
                column = jnp.sum(jnp.where(rec_row, amounts, 0.0), axis=1, keepdims=True)
                rinj[t, p] = jnp.where(lane == REC_DEPTH, column, 0.0)
            return carry

        lax.fori_loop(0, cells_x, plane, 0)

    def set_zeros():
        for way in (UP, DOWN):
            @pl.when(jnp.logical_not(has["gx", 1 - way]))
            def _(way=way):
                def fill(e, carry):
                    px[e, :, pl.ds(0 if way == UP else 4 + cells_x, 4)] = jnp.zeros((3, 4, cells_y, depth), jnp.float32)
                    return carry
                lax.fori_loop(0, 8, fill, 0)

            @pl.when(jnp.logical_not(has["gy", 1 - way]))
            def _(way=way):
                def fill(e, carry):
                    yr[e, way] = jnp.zeros(yr.shape[2:], jnp.float32)
                    return carry
                lax.fori_loop(0, 8, fill, 0)

    def x_copy(e, way, c, peer):
        n = layers(e, way, c)
        if way == UP:
            source, target = pl.ds(4 + cells_x - n, n), pl.ds(4 - n, n)
        else:
            source, target = pl.ds(4, n), pl.ds(4 + cells_x, n)
        return pltpu.make_async_remote_copy(
            px.at[e, c, source], px.at[e, c, target], xs_sem.at[e, way, c], xr_sem.at[e, way, c],
            device_id=neighbour("gx", peer), device_id_type=MESH,
        )

    odd_block = lax.rem(gx, 2)
    is_near = {UP: odd_block == 0, DOWN: odd_block == 1}

    def x_side(near, way):
        there = is_near[way] if near else jnp.logical_not(is_near[way])
        return jnp.logical_and(there, has["gx", way])

    def send_x(e, near):
        for way in (UP, DOWN):
            @pl.when(x_side(near, way))
            def _(way=way):
                for c in range(3):
                    x_copy(e, way, c, way).start()

    def sent_x(e, near):
        for way in (UP, DOWN):
            @pl.when(x_side(near, way))
            def _(way=way):
                for c in range(3):
                    x_copy(e, way, c, way).wait_send()

    def receive_x(e, near):
        for way in (UP, DOWN):
            @pl.when(x_side(near, 1 - way))
            def _(way=way):
                for c in range(3):
                    x_copy(e, way, c, 1 - way).wait_recv()

    half = pairs // 2
    part_of = {True: 1 - odd_block, False: odd_block}
    tiles = ys.shape[2] // 2

    def y_copy(e, way, near, peer):
        part = pl.ds(part_of[near] * tiles, tiles)
        k = 0 if near else 1
        return pltpu.make_async_remote_copy(
            ys.at[e, way, part], yr.at[e, way, part], ys_sem.at[e, way, k], yr_sem.at[e, way, k],
            device_id=neighbour("gy", peer), device_id_type=MESH,
        )

    def send_y(e, near):
        for way in (UP, DOWN):
            @pl.when(has["gy", way])
            def _(way=way):
                y_copy(e, way, near, way).start()

    def sent_y(e, near):
        for way in (UP, DOWN):
            @pl.when(has["gy", way])
            def _(way=way):
                y_copy(e, way, near, way).wait_send()

    def receive_y(e, near):
        for way in (UP, DOWN):
            @pl.when(has["gy", 1 - way])
            def _(way=way):
                y_copy(e, way, near, 1 - way).wait_recv()

        def unpack(i, carry):
            q = part_of[near] * half + i
            for odd in range(2):
                p = 2 * q + odd
                for c in range(3):
                    tile, rows4 = slot(c, q, odd)
                    py[e, c, p, pl.ds(4, 4), :] = yr[e, UP, tile, rows4, :]
                    py[e, c, p, pl.ds(8 + cells_y, 4), :] = yr[e, DOWN, tile, rows4, :]
            return carry

        lax.fori_loop(0, half, unpack, 0)

    def slot(c, q, odd):
        start, inside = lax.div(q, half) * tiles, lax.rem(q, half)
        if c < 2:
            return start + 2 * inside + odd, pl.ds(4 * c, 4)
        return start + 2 * half + inside, pl.ds(4 * odd, 4)

    def pack(e, c, q, odd, value):
        tile, part = slot(c, q, odd)
        ys[e, UP, tile, part, :] = value[cells_y - 4:]
        ys[e, DOWN, tile, part, :] = value[:4]

    def store_y(e, c, q, odd, value):
        py[e, c, 2 * q + odd, rows, :] = value
        pack(e, c, q, odd, value)

    def by_plane(body):
        def step(q, carry):
            for odd in range(2):
                body(q, odd, 2 * q + odd)
            return carry
        lax.fori_loop(0, pairs, step, 0)

    def stage(e, body, target=None):
        receive_y(e, True)
        receive_x(e, True)

        def step(i, carry):
            @pl.when(i == half)
            def _():
                if target is not None:
                    send_y(target, True)
                    send_x(target, True)
                receive_y(e, False)
                receive_x(e, False)

            q = lax.rem(i + half * part_of[True], pairs)
            for odd in range(2):
                body(q, odd, 2 * q + odd)
            return carry

        lax.fori_loop(0, pairs, step, 0)
        if target is not None:
            send_x(target, False)
            send_y(target, False)

    def diff_x(e, c, p, forward):
        return diff(lambda k: px[e, c, p + (4 + k)], forward)

    def diff_y(e, c, p, forward):
        return diff(lambda k: py[e, c, p, pl.ds(8 + k, cells_y), :], forward)

    def diff_z(value, forward):
        def at(k):
            if k == 0:
                return value
            moved = pltpu.roll(value, (-k) % depth, 1)
            return jnp.where(lane < depth - k if k > 0 else lane >= -k, moved, 0.0)
        return diff(at, forward)

    def center_x(e, c, p):
        return px[e, c, p + 4]

    def center_y(e, c, p):
        return py[e, c, p, rows, :]

    def stresses(e, p):
        return (
            center_x(e, 0, p), center_y(e, 0, p), szz[e, p],
            center_x(e, 1, p), center_x(e, 2, p), center_y(e, 2, p),
        )

    def velocity_half(e, target, before):
        def body(q, odd, p):
            s = stresses(e, p)
            force = (
                diff_x(e, 0, p, True) + diff_y(e, 1, p, False) + diff_z(s[4], False),
                diff_x(e, 1, p, False) + diff_y(e, 0, p, True) + diff_z(s[5], False),
                diff_x(e, 2, p, False) + diff_y(e, 2, p, False) + diff_z(s[2], True),
            )
            scaled = TIME_STEP * buo[p]
            for c in range(3):
                value = damp[p] * (before(c, p) + scaled * force[c])
                px[target, c, p + 4] = value
                store_y(target, c, q, odd, value)
        return body

    def strain(e, p):
        vx, vy, vz = (center_x(e, c, p) for c in range(3))
        return (
            diff_x(e, 0, p, False),
            diff_y(e, 1, p, False),
            diff_z(vz, False),
            diff_y(e, 0, p, True) + diff_x(e, 1, p, True),
            diff_z(vx, True) + diff_x(e, 2, p, True),
            diff_z(vy, True) + diff_y(e, 2, p, True),
        )

    def stress_half(e, rates, p):
        s = stresses(e, p)
        normal = lam[p] * (rates[0] + rates[1] + rates[2])
        shear = TIME_STEP * mu[p]
        return [
            damp[p] * (s[k] + (TIME_STEP * normal + 2.0 * shear * rates[k])) for k in range(3)
        ] + [damp[p] * (s[k] + shear * rates[k]) for k in range(3, 6)]

    def store_stress(e, q, odd, p, s):
        for c, k in enumerate((0, 3, 4)):
            px[e, c, p + 4] = s[k]
        for c, k in enumerate((1, 3, 5)):
            store_y(e, c, q, odd, s[k])
        szz[e, p] = s[2]

    def forward_stress(q, odd, p):
        rates = strain(FV1, p)
        for k in range(6):
            rates1[k, p] = rates[k]
        s = stress_half(FS0, rates, p)
        for k in range(3):
            s[k] = s[k] + src[p]
        store_stress(FS1, q, odd, p, s)

    def adjoint_stress(q, odd, p):
        store_stress(AS1, q, odd, p, stress_half(AS0, strain(AV1, p), p))

    def adjoint_velocity(e, t, c, p):
        value = center_x(e, c, p)
        return value + rinj[t, p] if c == 2 else value

    def density(q, odd, p):
        total = None
        for c in range(3):
            one = center_x(FV1, c, p)
            term = (
                adjoint_velocity(AV1, 0, c, p) * (center_x(FV2, c, p) - one)
                + adjoint_velocity(AV0, 1, c, p) * (one - vel0[0, c, p])
            )
            total = term if total is None else total + term
        g_rho[p] = total / TIME_STEP

    def image(rates, s):
        lam_term = (rates[0] + rates[1] + rates[2]) * (s[0] + s[1] + s[2])
        normal = rates[0] * s[0] + rates[1] * s[1] + rates[2] * s[2]
        return lam_term, 2.0 * normal + rates[3] * s[3] + rates[4] * s[4] + rates[5] * s[5]

    def image_one(q, odd, p):
        g_lam[p], g_mu[p] = image(strain(FV2, p), stresses(AS1, p))

    def image_two(q, odd, p):
        s = stress_half(AS1, strain(AV0, p), p)
        lam_term, mu_term = image([rates1[k, p] for k in range(6)], s)
        g_lam[p] = g_lam[p] + lam_term
        g_mu[p] = g_mu[p] + mu_term

    forward_one = velocity_half(FS0, FV1, lambda c, p: vel0[0, c, p])
    adjoint_one = velocity_half(AS0, AV1, lambda c, p: vel0[1, c, p])
    forward_two = velocity_half(FS1, FV2, lambda c, p: center_x(FV1, c, p))
    adjoint_two = velocity_half(AS1, AV0, lambda c, p: adjoint_velocity(AV1, 0, c, p))

    def send_first_y(e):
        for c in range(3):
            loads["py", e, c].wait()

        def first(q, odd, p):
            for c in range(3):
                pack(e, c, q, odd, center_y(e, c, p))
        by_plane(first)
        send_y(e, True)
        send_y(e, False)

    for c in range(3):
        loads["px", FS0, c].wait()
    pl.semaphore_wait(barrier, sum(there.astype(jnp.int32) for there in has.values()))
    send_x(FS0, False)
    send_x(FS0, True)
    send_first_y(FS0)
    set_damping()
    set_zeros()
    set_injections()
    for name, copy in loads.items():
        if name[0] not in ("px", "py") or name[:2] == ("px", AS0):
            copy.wait()
    sent_x(FS0, False)
    send_x(AS0, False)
    send_x(AS0, True)
    send_first_y(AS0)

    stage(FS0, forward_one, FV1)
    stage(AS0, adjoint_one, AV1)
    stage(FV1, forward_stress, FS1)
    stage(AV1, adjoint_stress, AS1)
    stage(FS1, forward_two, FV2)
    stage(AS1, adjoint_two, AV0)
    by_plane(density)
    stage(FV2, image_one)
    stage(AV0, image_two)

    for e in range(8):
        if e != FS0:
            sent_x(e, False)
        sent_x(e, True)
        sent_y(e, True)
        sent_y(e, False)


def local(
    forward_state, adjoint_state, lame_lambda, lame_mu, buoyancy,
    source_x, source_y, source_z, source_wavelet,
    receiver_x, receiver_y, receiver_residual, absorb_width,
):
    block = buoyancy.shape
    cells_x, cells_y, depth = block
    f32 = jnp.float32
    hbm, vmem, smem = (pl.BlockSpec(memory_space=m) for m in (pl.ANY, pltpu.VMEM, pltpu.SMEM))
    dma = pltpu.SemaphoreType.DMA
    packed = (8, 2, cells_x + cells_x // 2, 8, depth)
    grads = pl.pallas_call(
        kernel,
        out_shape=jax.ShapeDtypeStruct((3,) + block, f32),
        in_specs=[hbm] * 5 + [smem] * 5 + [vmem] * 3,
        out_specs=vmem,
        scratch_shapes=[
            pltpu.VMEM((8, 3, cells_x + 8, cells_y, depth), f32),
            pltpu.VMEM((8, 3, cells_x, cells_y + 16, depth), f32),
            pltpu.VMEM(packed, f32),
            pltpu.VMEM(packed, f32),
            pltpu.VMEM((8,) + block, f32),
            pltpu.VMEM((2, 3) + block, f32),
            pltpu.VMEM(block, f32),
            pltpu.VMEM(block, f32),
            pltpu.VMEM(block, f32),
            pltpu.VMEM(block, f32),
            pltpu.VMEM(block, f32),
            pltpu.VMEM((2,) + block, f32),
            pltpu.VMEM((6,) + block, f32),
            dma((19,)),
            dma((8, 2, 3)),
            dma((8, 2, 3)),
            dma((8, 2, 2)),
            dma((8, 2, 2)),
        ],
        compiler_params=pltpu.CompilerParams(
            collective_id=0, has_side_effects=True, vmem_limit_bytes=60 * 1024 * 1024
        ),
        name="window",
    )(
        forward_state, adjoint_state, lame_lambda, lame_mu, buoyancy,
        source_x, source_y, source_z, source_wavelet, absorb_width,
        receiver_x.reshape(1, -1), receiver_y.reshape(1, -1), receiver_residual,
    )
    return grads[0], grads[1], grads[2]


def solution(mesh):
    volume = P("gx", "gy", None)
    state = P(None, "gx", "gy", None)
    return jax.shard_map(
        local,
        mesh=mesh,
        in_specs=(state, state, volume, volume, volume) + (P(),) * 8,
        out_specs=(volume, volume, volume),
        check_vma=False,
    )
```

```python
import jax
import jax.numpy as jnp
from jax import lax
from jax.experimental import pallas as pl
from jax.experimental.pallas import tpu as pltpu
from jax.sharding import PartitionSpec as P

REC_DEPTH = 6
COEFS = (1225.0 / 1024.0, -245.0 / 3072.0, 49.0 / 5120.0, -5.0 / 7168.0)
TIME_STEP = 0.2
DAMPING = 0.3
MESH = pl.DeviceIdType.MESH

FS0, FV1, FS1, FV2, AS0, AV1, AS1, AV0 = range(8)
VELOCITY = (FV1, FV2, AV1, AV0)
UP, DOWN = 0, 1


def layers(e, way, c):
    backward = (c == 0) if e in VELOCITY else (c != 0)
    return 4 if backward == (way == UP) else 3


def diff(load, forward):
    total = None
    for order, coef in enumerate(COEFS, 1):
        high, low = (order, 1 - order) if forward else (order - 1, -order)
        term = coef * (load(high) - load(low))
        total = term if total is None else total + term
    return total


def kernel(
    fwd, adj, lam_in, mu_in, buo_in, src_x, src_y, src_z, src_w, width_in, rec_x, rec_y, residual,
    grads,
    px, py, ys, yr, szz, vel0, lam, mu, buo, damp, src, rinj, rates1,
    load_sem, xs_sem, xr_sem, ys_sem, yr_sem,
):
    g_lam, g_mu, g_rho = (grads.at[k] for k in range(3))
    gx, gy = lax.axis_index("gx"), lax.axis_index("gy")
    nx, ny = lax.axis_size("gx"), lax.axis_size("gy")
    cells_x, cells_y, depth = buo.shape
    pairs = cells_x // 2
    anchor_x, anchor_y = gx * cells_x, gy * cells_y
    total_x, total_y = nx * cells_x, ny * cells_y
    has = {("gx", UP): gx < nx - 1, ("gx", DOWN): gx > 0, ("gy", UP): gy < ny - 1, ("gy", DOWN): gy > 0}
    place = {"gx": gx, "gy": gy}

    def neighbour(axis, way):
        return {axis: place[axis] + (1 if way == UP else -1)}

    loads = {}

    def load(name, source, target):
        copy = pltpu.make_async_copy(source, target, load_sem.at[len(loads)])
        copy.start()
        loads[name] = copy

    middle, rows = pl.ds(4, cells_x), pl.ds(8, cells_y)
    for chain, (state, e) in enumerate(((fwd, FS0), (adj, AS0))):
        for c, k in enumerate((3, 6, 7)):
            load(("px", e, c), state.at[k], px.at[e, c, middle])
        for c, k in enumerate((4, 6, 8)):
            load(("py", e, c), state.at[k], py.at[e, c, :, rows])
    for chain, (state, e) in enumerate(((fwd, FS0), (adj, AS0))):
        load(("szz", e), state.at[5], szz.at[e])
        load(("vel", e), state.at[pl.ds(0, 3)], vel0.at[chain])
    load("buo", buo_in, buo)
    load("lam", lam_in, lam)
    load("mu", mu_in, mu)

    barrier = pltpu.get_barrier_semaphore()
    for (axis, way), there in has.items():
        @pl.when(there)
        def _(axis=axis, way=way):
            pl.semaphore_signal(barrier, inc=1, device_id=neighbour(axis, way), device_id_type=MESH)

    row = lax.broadcasted_iota(jnp.int32, (cells_y, depth), 0)
    lane = lax.broadcasted_iota(jnp.int32, (cells_y, depth), 1)
    coord_y = anchor_y + row

    def set_damping():
        width = width_in[0].astype(jnp.float32)

        def taper(dist):
            frac = jnp.maximum(width - dist.astype(jnp.float32), 0.0) / width
            return jnp.exp(-DAMPING * frac * frac)

        taper_y = taper(jnp.minimum(coord_y, total_y - 1 - coord_y))
        taper_z = taper(depth - 1 - lane)

        def plane(p, carry):
            coord_x = jnp.zeros((cells_y, depth), jnp.int32) + (anchor_x + p)
            damp[p] = taper(jnp.minimum(coord_x, total_x - 1 - coord_x)) * taper_y * taper_z
            return carry

        lax.fori_loop(0, cells_x, plane, 0)

    def set_injections():
        rec_row = anchor_y + lax.broadcasted_iota(jnp.int32, (cells_y, rec_x.shape[1]), 0) == rec_y[...]

        def plane(p, carry):
            total = jnp.zeros((cells_y, depth), jnp.float32)
            for s in range(src_x.shape[0]):
                amount = jnp.where(src_x[s] == anchor_x + p, TIME_STEP * src_w[s], 0.0)
                hit = (coord_y == src_y[s]) & (lane == src_z[s])
                total = total + jnp.where(hit, amount, 0.0)
            src[p] = total
            for t in range(2):
                amounts = jnp.where(rec_x[...] == anchor_x + p, TIME_STEP * residual[pl.ds(t, 1), :], 0.0)
                column = jnp.sum(jnp.where(rec_row, amounts, 0.0), axis=1, keepdims=True)
                rinj[t, p] = jnp.where(lane == REC_DEPTH, column, 0.0)
            return carry

        lax.fori_loop(0, cells_x, plane, 0)

    def set_zeros():
        for way in (UP, DOWN):
            @pl.when(jnp.logical_not(has["gx", 1 - way]))
            def _(way=way):
                def fill(e, carry):
                    px[e, :, pl.ds(0 if way == UP else 4 + cells_x, 4)] = jnp.zeros((3, 4, cells_y, depth), jnp.float32)
                    return carry
                lax.fori_loop(0, 8, fill, 0)

            @pl.when(jnp.logical_not(has["gy", 1 - way]))
            def _(way=way):
                def fill(e, carry):
                    yr[e, way] = jnp.zeros(yr.shape[2:], jnp.float32)
                    return carry
                lax.fori_loop(0, 8, fill, 0)

    def x_copy(e, way, c, peer):
        n = layers(e, way, c)
        if way == UP:
            source, target = pl.ds(4 + cells_x - n, n), pl.ds(4 - n, n)
        else:
            source, target = pl.ds(4, n), pl.ds(4 + cells_x, n)
        return pltpu.make_async_remote_copy(
            px.at[e, c, source], px.at[e, c, target], xs_sem.at[e, way, c], xr_sem.at[e, way, c],
            device_id=neighbour("gx", peer), device_id_type=MESH,
        )

    odd_block = lax.rem(gx, 2)
    is_near = {UP: odd_block == 0, DOWN: odd_block == 1}

    def x_side(near, way):
        there = is_near[way] if near else jnp.logical_not(is_near[way])
        return jnp.logical_and(there, has["gx", way])

    def send_x(e, near):
        for way in (UP, DOWN):
            @pl.when(x_side(near, way))
            def _(way=way):
                for c in range(3):
                    x_copy(e, way, c, way).start()

    def sent_x(e, near):
        for way in (UP, DOWN):
            @pl.when(x_side(near, way))
            def _(way=way):
                for c in range(3):
                    x_copy(e, way, c, way).wait_send()

    def receive_x(e, near):
        for way in (UP, DOWN):
            @pl.when(x_side(near, 1 - way))
            def _(way=way):
                for c in range(3):
                    x_copy(e, way, c, 1 - way).wait_recv()

    half = pairs // 2
    part_of = {True: 1 - odd_block, False: odd_block}
    tiles = ys.shape[2] // 2

    def y_copy(e, way, near, peer):
        part = pl.ds(part_of[near] * tiles, tiles)
        k = 0 if near else 1
        return pltpu.make_async_remote_copy(
            ys.at[e, way, part], yr.at[e, way, part], ys_sem.at[e, way, k], yr_sem.at[e, way, k],
            device_id=neighbour("gy", peer), device_id_type=MESH,
        )

    def send_y(e, near):
        for way in (UP, DOWN):
            @pl.when(has["gy", way])
            def _(way=way):
                y_copy(e, way, near, way).start()

    def sent_y(e, near):
        for way in (UP, DOWN):
            @pl.when(has["gy", way])
            def _(way=way):
                y_copy(e, way, near, way).wait_send()

    def receive_y(e, near):
        for way in (UP, DOWN):
            @pl.when(has["gy", 1 - way])
            def _(way=way):
                y_copy(e, way, near, 1 - way).wait_recv()

        def unpack(i, carry):
            q = part_of[near] * half + i
            for odd in range(2):
                p = 2 * q + odd
                for c in range(3):
                    tile, rows4 = slot(c, q, odd)
                    py[e, c, p, pl.ds(4, 4), :] = yr[e, UP, tile, rows4, :]
                    py[e, c, p, pl.ds(8 + cells_y, 4), :] = yr[e, DOWN, tile, rows4, :]
            return carry

        lax.fori_loop(0, half, unpack, 0)

    def slot(c, q, odd):
        start, inside = lax.div(q, half) * tiles, lax.rem(q, half)
        if c < 2:
            return start + 2 * inside + odd, pl.ds(4 * c, 4)
        return start + 2 * half + inside, pl.ds(4 * odd, 4)

    def pack(e, c, q, odd, value):
        tile, part = slot(c, q, odd)
        ys[e, UP, tile, part, :] = value[cells_y - 4:]
        ys[e, DOWN, tile, part, :] = value[:4]

    def store_y(e, c, q, odd, value):
        py[e, c, 2 * q + odd, rows, :] = value
        pack(e, c, q, odd, value)

    def by_plane(body):
        def step(q, carry):
            for odd in range(2):
                body(q, odd, 2 * q + odd)
            return carry
        lax.fori_loop(0, pairs, step, 0)

    def stage(e, body, target=None):
        receive_y(e, True)
        receive_x(e, True)

        def step(i, carry):
            @pl.when(i == half)
            def _():
                if target is not None:
                    send_y(target, True)
                    send_x(target, True)
                receive_y(e, False)
                receive_x(e, False)

            q = lax.rem(i + half * part_of[True], pairs)
            for odd in range(2):
                body(q, odd, 2 * q + odd)
            return carry

        lax.fori_loop(0, pairs, step, 0)
        if target is not None:
            send_x(target, False)
            send_y(target, False)

    def diff_x(e, c, p, forward):
        return diff(lambda k: px[e, c, p + (4 + k)], forward)

    def diff_y(e, c, p, forward):
        return diff(lambda k: py[e, c, p, pl.ds(8 + k, cells_y), :], forward)

    def diff_z(value, forward):
        def at(k):
            if k == 0:
                return value
            moved = pltpu.roll(value, (-k) % depth, 1)
            return jnp.where(lane < depth - k if k > 0 else lane >= -k, moved, 0.0)
        return diff(at, forward)

    def center_x(e, c, p):
        return px[e, c, p + 4]

    def center_y(e, c, p):
        return py[e, c, p, rows, :]

    def stresses(e, p):
        return (
            center_x(e, 0, p), center_y(e, 0, p), szz[e, p],
            center_x(e, 1, p), center_x(e, 2, p), center_y(e, 2, p),
        )

    def velocity_half(e, target, before):
        def body(q, odd, p):
            s = stresses(e, p)
            force = (
                diff_x(e, 0, p, True) + diff_y(e, 1, p, False) + diff_z(s[4], False),
                diff_x(e, 1, p, False) + diff_y(e, 0, p, True) + diff_z(s[5], False),
                diff_x(e, 2, p, False) + diff_y(e, 2, p, False) + diff_z(s[2], True),
            )
            scaled = TIME_STEP * buo[p]
            for c in range(3):
                value = damp[p] * (before(c, p) + scaled * force[c])
                px[target, c, p + 4] = value
                store_y(target, c, q, odd, value)
        return body

    def strain(e, p):
        vx, vy, vz = (center_x(e, c, p) for c in range(3))
        return (
            diff_x(e, 0, p, False),
            diff_y(e, 1, p, False),
            diff_z(vz, False),
            diff_y(e, 0, p, True) + diff_x(e, 1, p, True),
            diff_z(vx, True) + diff_x(e, 2, p, True),
            diff_z(vy, True) + diff_y(e, 2, p, True),
        )

    def stress_half(e, rates, p):
        s = stresses(e, p)
        normal = lam[p] * (rates[0] + rates[1] + rates[2])
        shear = TIME_STEP * mu[p]
        return [
            damp[p] * (s[k] + (TIME_STEP * normal + 2.0 * shear * rates[k])) for k in range(3)
        ] + [damp[p] * (s[k] + shear * rates[k]) for k in range(3, 6)]

    def store_stress(e, q, odd, p, s):
        for c, k in enumerate((0, 3, 4)):
            px[e, c, p + 4] = s[k]
        for c, k in enumerate((1, 3, 5)):
            store_y(e, c, q, odd, s[k])
        szz[e, p] = s[2]

    def forward_stress(q, odd, p):
        rates = strain(FV1, p)
        for k in range(6):
            rates1[k, p] = rates[k]
        s = stress_half(FS0, rates, p)
        for k in range(3):
            s[k] = s[k] + src[p]
        store_stress(FS1, q, odd, p, s)

    def adjoint_stress(q, odd, p):
        store_stress(AS1, q, odd, p, stress_half(AS0, strain(AV1, p), p))

    def adjoint_velocity(e, t, c, p):
        value = center_x(e, c, p)
        return value + rinj[t, p] if c == 2 else value

    def density(q, odd, p):
        total = None
        for c in range(3):
            one = center_x(FV1, c, p)
            term = (
                adjoint_velocity(AV1, 0, c, p) * (center_x(FV2, c, p) - one)
                + adjoint_velocity(AV0, 1, c, p) * (one - vel0[0, c, p])
            )
            total = term if total is None else total + term
        g_rho[p] = total / TIME_STEP

    def image(rates, s):
        lam_term = (rates[0] + rates[1] + rates[2]) * (s[0] + s[1] + s[2])
        normal = rates[0] * s[0] + rates[1] * s[1] + rates[2] * s[2]
        return lam_term, 2.0 * normal + rates[3] * s[3] + rates[4] * s[4] + rates[5] * s[5]

    def image_one(q, odd, p):
        g_lam[p], g_mu[p] = image(strain(FV2, p), stresses(AS1, p))

    def image_two(q, odd, p):
        s = stress_half(AS1, strain(AV0, p), p)
        lam_term, mu_term = image([rates1[k, p] for k in range(6)], s)
        g_lam[p] = g_lam[p] + lam_term
        g_mu[p] = g_mu[p] + mu_term

    forward_one = velocity_half(FS0, FV1, lambda c, p: vel0[0, c, p])
    adjoint_one = velocity_half(AS0, AV1, lambda c, p: vel0[1, c, p])
    forward_two = velocity_half(FS1, FV2, lambda c, p: center_x(FV1, c, p))
    adjoint_two = velocity_half(AS1, AV0, lambda c, p: adjoint_velocity(AV1, 0, c, p))

    def ready(e):
        for c in range(3):
            loads["py", e, c].wait()

        def first(q, odd, p):
            for c in range(3):
                pack(e, c, q, odd, center_y(e, c, p))
        by_plane(first)
        for c in range(3):
            loads["px", e, c].wait()

    ready(FS0)
    ready(AS0)
    set_damping()
    pl.semaphore_wait(barrier, sum(there.astype(jnp.int32) for there in has.values()))
    def send_first(e):
        send_x(e, False)
        send_y(e, True)
        send_x(e, True)
        send_y(e, False)

    send_first(FS0)
    send_first(AS0)
    set_zeros()
    set_injections()
    for name, copy in loads.items():
        if name[0] not in ("px", "py"):
            copy.wait()

    stage(FS0, forward_one, FV1)
    stage(AS0, adjoint_one, AV1)
    stage(FV1, forward_stress, FS1)
    stage(AV1, adjoint_stress, AS1)
    stage(FS1, forward_two, FV2)
    stage(AS1, adjoint_two, AV0)
    by_plane(density)
    stage(FV2, image_one)
    stage(AV0, image_two)

    for e in range(8):
        sent_x(e, False)
        sent_x(e, True)
        sent_y(e, True)
        sent_y(e, False)


def local(
    forward_state, adjoint_state, lame_lambda, lame_mu, buoyancy,
    source_x, source_y, source_z, source_wavelet,
    receiver_x, receiver_y, receiver_residual, absorb_width,
):
    block = buoyancy.shape
    cells_x, cells_y, depth = block
    f32 = jnp.float32
    hbm, vmem, smem = (pl.BlockSpec(memory_space=m) for m in (pl.ANY, pltpu.VMEM, pltpu.SMEM))
    dma = pltpu.SemaphoreType.DMA
    packed = (8, 2, cells_x + cells_x // 2, 8, depth)
    grads = pl.pallas_call(
        kernel,
        out_shape=jax.ShapeDtypeStruct((3,) + block, f32),
        in_specs=[hbm] * 5 + [smem] * 5 + [vmem] * 3,
        out_specs=vmem,
        scratch_shapes=[
            pltpu.VMEM((8, 3, cells_x + 8, cells_y, depth), f32),
            pltpu.VMEM((8, 3, cells_x, cells_y + 16, depth), f32),
            pltpu.VMEM(packed, f32),
            pltpu.VMEM(packed, f32),
            pltpu.VMEM((8,) + block, f32),
            pltpu.VMEM((2, 3) + block, f32),
            pltpu.VMEM(block, f32),
            pltpu.VMEM(block, f32),
            pltpu.VMEM(block, f32),
            pltpu.VMEM(block, f32),
            pltpu.VMEM(block, f32),
            pltpu.VMEM((2,) + block, f32),
            pltpu.VMEM((6,) + block, f32),
            dma((19,)),
            dma((8, 2, 3)),
            dma((8, 2, 3)),
            dma((8, 2, 2)),
            dma((8, 2, 2)),
        ],
        compiler_params=pltpu.CompilerParams(
            collective_id=0, has_side_effects=True, vmem_limit_bytes=60 * 1024 * 1024
        ),
        name="window",
    )(
        forward_state, adjoint_state, lame_lambda, lame_mu, buoyancy,
        source_x, source_y, source_z, source_wavelet, absorb_width,
        receiver_x.reshape(1, -1), receiver_y.reshape(1, -1), receiver_residual,
    )
    return grads[0], grads[1], grads[2]


def solution(mesh):
    volume = P("gx", "gy", None)
    state = P(None, "gx", "gy", None)
    return jax.shard_map(
        local,
        mesh=mesh,
        in_specs=(state, state, volume, volume, volume) + (P(),) * 8,
        out_specs=(volume, volume, volume),
        check_vma=False,
    )
```
